128 devices in a mesh: gx: 4 (over z), gy: 4 (over x), gz: 8 (over y, core).
Axes of the slice: x: 4, y: 4, z: 4, core: 2. Of those that a mesh axis runs over, the one named last changes fastest.
Arguments:
- density_blocks: bfloat16 [4096, 128, 128], P(('gx', 'gy', 'gz')), may hold values from -0.00625 to 0.00625
- orbital_values: bfloat16 [64, 64, 128, 1280], P('gx', 'gy', 'gz'), may hold values from -11 to 11
- pair_index: int32 [128, 100], P(('gx', 'gy', 'gz')), may hold values from 0 to 4095, as said below
Outputs:
- potential_blocks: float32 [4096, 128, 128], P(('gx', 'gy', 'gz'))
- potential: float32 [64, 64, 128], P('gx', 'gy', 'gz')
The draws below stay inside these ranges and needn't reach their ends.
Inputs may be any that keep to these rules, and one draw needn't show every extreme that they name: `pair_index`: A domain's 100 entries are distinct. Each domain names at most 2 blocks held by one device, and exactly 2 for some holder.
All inputs are finite; a program needn't handle non-finite values.
Results may differ from the reference program's by a relative error of at most 0.0034.
Values may be sent and summed in bfloat16 or wider, within the bound.
A program may use at most 128 MiB of HBM per device.

```python
import jax
import jax.numpy as jnp
from jax import lax

BLOCK = 128
ORB_BLOCKS = 10
LOCAL_ORB = 1280
NPAIR = 100
SPREAD = 50
NNZ_DEV = 32
NNZ = 4096
CX = 16
CY = 16
CZ = 16
NX = 64
NY = 64
NZ = 128
NPRE = 2
NCOARSE = 4
NPOST = 2
N_GX = 4
N_GY = 4
N_GZ = 8
DEVICES = 128


def shuffled_holders(one_key):
    return jax.random.permutation(one_key, DEVICES)


def draw_pair_index(key, part):
    key = jax.random.fold_in(key, 7)
    holder_keys = jax.random.split(jax.random.fold_in(key, 1), DEVICES)
    holders = jax.vmap(shuffled_holders)(holder_keys)[:, :SPREAD]
    offsets = jax.random.randint(jax.random.fold_in(key, 2), (DEVICES, SPREAD), 0, NNZ_DEV)
    order = jnp.arange(NPAIR, dtype=jnp.int32)
    column = order % SPREAD
    layer = order // SPREAD
    holder = holders[:, column]
    slot = (offsets[:, column] + layer[None, :]) % NNZ_DEV
    return (holder * NNZ_DEV + slot).astype(jnp.int32)


def draw_density_blocks(key, part):
    key = jax.random.fold_in(key, 11)
    identity = jnp.eye(BLOCK, dtype=jnp.float32)[None]
    raw = jnp.clip(jax.random.normal(key, (NNZ, BLOCK, BLOCK), jnp.float32), -6.0, 6.0)
    offset = 1.5
    return ((raw + offset * identity) / LOCAL_ORB).astype(jnp.bfloat16)


def draw_orbital_values(key, part):
    key = jax.random.fold_in(key, 13)
    rise_x = jnp.arange(NX, dtype=jnp.float32) / max(NX - 1, 1)
    squared = (1.0 + 2.0 * rise_x)[:, None, None]
    raw = jnp.clip(jax.random.normal(key, (NX, NY, NZ, LOCAL_ORB), jnp.float32), -6.0, 6.0)
    return (raw * jnp.sqrt(squared)[..., None]).astype(jnp.bfloat16)


def setup_inputs(seed: int = 0) -> dict:
    arg_keys = jax.random.split(jax.random.key(seed), 4)
    return {
        "density_blocks": draw_density_blocks(jax.random.fold_in(arg_keys[3], 71), 0),
        "orbital_values": draw_orbital_values(jax.random.fold_in(arg_keys[3], 71), 0),
        "pair_index": draw_pair_index(jax.random.fold_in(arg_keys[3], 71), 0),
    }


OMEGA = 0.6
SCREEN = 0.05


def apply_operator(field, diag):
    beside = jnp.roll(field, 1, 0) + jnp.roll(field, -1, 0)
    beside = beside + jnp.roll(field, 1, 1) + jnp.roll(field, -1, 1)
    beside = beside + jnp.roll(field, 1, 2) + jnp.roll(field, -1, 2)
    return diag * field - beside


def relax(field, source, diag):
    return field + OMEGA * (source - apply_operator(field, diag)) / diag


def domain_cells(orbital_values, domain):
    first = domain // (N_GY * N_GZ)
    second = (domain // N_GZ) % N_GY
    third = domain % N_GZ
    zero = domain * 0
    piece = lax.dynamic_slice(orbital_values, (first * CX, second * CY, third * CZ, zero), (CX, CY, CZ, LOCAL_ORB))
    return piece.reshape(CX * CY * CZ, LOCAL_ORB), (first * CX, second * CY, third * CZ)


def reference(density_blocks, orbital_values, pair_index):
    ndomain = N_GX * N_GY * N_GZ
    domains = jnp.arange(ndomain, dtype=jnp.int32)

    def collocate(domain):
        orbitals, corner = domain_cells(orbital_values, domain)
        blocks = density_blocks[pair_index[domain]]
        local_matrix = blocks.reshape(ORB_BLOCKS, ORB_BLOCKS, BLOCK, BLOCK).transpose(0, 2, 1, 3).reshape(LOCAL_ORB, LOCAL_ORB)
        product = jnp.dot(orbitals, local_matrix, preferred_element_type=jnp.float32)
        return jnp.sum(orbitals.astype(jnp.float32) * product, axis=1).reshape(CX, CY, CZ)

    pieces = lax.map(collocate, domains)
    density = pieces.reshape(N_GX, N_GY, N_GZ, CX, CY, CZ).transpose(0, 3, 1, 4, 2, 5).reshape(NX, NY, NZ)
    source = density - jnp.sum(density) / (NX * NY * NZ)
    fine_diag = 6.0 + SCREEN
    coarse_diag = 6.0 + 4.0 * SCREEN
    field = jnp.zeros((NX, NY, NZ), jnp.float32)
    for sweep_index in range(NPRE):
        field = relax(field, source, fine_diag)
    residual = source - apply_operator(field, fine_diag)
    coarse_source = 4.0 * jnp.mean(residual.reshape(NX // 2, 2, NY // 2, 2, NZ // 2, 2), axis=(1, 3, 5))
    correction = jnp.zeros_like(coarse_source)
    for sweep_index in range(NCOARSE):
        correction = relax(correction, coarse_source, coarse_diag)
    field = field + jnp.repeat(jnp.repeat(jnp.repeat(correction, 2, 0), 2, 1), 2, 2)
    for sweep_index in range(NPOST):
        field = relax(field, source, fine_diag)
    potential = field
    scale = (CX * CY * CZ) ** -0.5

    def integrate(total, domain):
        orbitals, corner = domain_cells(orbital_values, domain)
        values = lax.dynamic_slice(potential, corner, (CX, CY, CZ)).reshape(-1)
        weighted = (values[:, None] * orbitals.astype(jnp.float32)).astype(jnp.bfloat16)
        matrix = lax.dot_general(orbitals, weighted, (((0,), (0,)), ((), ())), preferred_element_type=jnp.float32) * scale
        blocks = matrix.reshape(ORB_BLOCKS, BLOCK, ORB_BLOCKS, BLOCK).transpose(0, 2, 1, 3).reshape(NPAIR, BLOCK, BLOCK)
        blocks = blocks.astype(jnp.bfloat16).astype(jnp.float32)
        return total.at[pair_index[domain]].add(blocks), None

    start = jnp.zeros((NNZ, BLOCK, BLOCK), jnp.float32)
    potential_blocks, unused = lax.scan(integrate, start, domains)
    return potential_blocks, potential
```

```python
import functools

import jax
import jax.numpy as jnp
from jax import lax
from jax.experimental import pallas as pl
from jax.experimental.pallas import tpu as pltpu
from jax.sharding import PartitionSpec as P

MESH = pl.DeviceIdType.MESH
ORB_BLOCKS = 10
NPAIR = 100
BLOCK = 128
HALF = 64
NDEV = 128
NSLOT = 256
NNZ_DEV = 32
CELLS = 4096
LOCAL_ORB = 1280
CHUNK = 256
NCHUNK = CELLS // CHUNK
TOTAL_CELLS = 524288

OMEGA = 0.6
SCREEN = 0.05
FINE = 6.0 + SCREEN
COARSE = 6.0 + 4.0 * SCREEN
NPRE = 2
NCOARSE = 4
NPOST = 2


def constant_response():
    field = 0.0
    for _ in range(NPRE):
        field = field + OMEGA * (1.0 - (FINE - 6.0) * field) / FINE
    rest = 4.0 * (1.0 - (FINE - 6.0) * field)
    correction = 0.0
    for _ in range(NCOARSE):
        correction = correction + OMEGA * (rest - (COARSE - 6.0) * correction) / COARSE
    field = field + correction
    for _ in range(NPOST):
        field = field + OMEGA * (1.0 - (FINE - 6.0) * field) / FINE
    return field


def here():
    z = lax.axis_index("gz")
    return lax.axis_index("gx"), lax.axis_index("gy"), z // 2, z % 2


def beyond(offset):
    x, y, w, c = here()
    dx, dy, dw, dc = offset
    return (x + dx) % 4, (y + dy) % 4, ((w + dw) % 4) * 2 + (c + dc) % 2


def before(offset):
    dx, dy, dw, dc = offset
    return beyond((4 - dx, 4 - dy, 4 - dw, dc))


def offset_of(k):
    return k // 32, (k // 8) % 4, (k // 2) % 4, k % 2


def turn(i):
    a, b, e, c = i % 4, (i // 4) % 4, (i // 16) % 4, (i // 64 + i) % 2
    return a, (a + b) % 4, (a + e) % 4, c


def number(offset):
    dx, dy, dw, dc = offset
    return dx * 32 + dy * 8 + dw * 2 + dc


def remote(src, dst, send, recv, device):
    return pltpu.make_async_remote_copy(
        src_ref=src, dst_ref=dst, send_sem=send, recv_sem=recv,
        device_id=device, device_id_type=MESH,
    )


def beside(v, n, zlane):
    result = []
    for b in range(3):
        total = pltpu.roll(v[b], n, 0) + pltpu.roll(v[b], 48 - n, 0)
        total = total + pltpu.roll(v[b], 16 * n, 1) + pltpu.roll(v[b], 768 - 16 * n, 1)
        up = jnp.where(
            zlane >= 16 - n,
            pltpu.roll(v[(b + 1) % 3], 16 - n, 1),
            pltpu.roll(v[b], 768 - n, 1),
        )
        down = jnp.where(
            zlane < n,
            pltpu.roll(v[(b + 2) % 3], 768 - 16 + n, 1),
            pltpu.roll(v[b], n, 1),
        )
        result.append(total + up + down)
    return result


def pair_sums(r, row, lane):
    r = r + jnp.where(row % 2 == 0, pltpu.roll(r, 47, 0), pltpu.roll(r, 1, 0))
    r = r + jnp.where((lane // 16) % 2 == 0, pltpu.roll(r, 752, 1), pltpu.roll(r, 16, 1))
    return r + jnp.where(lane % 2 == 0, pltpu.roll(r, 767, 1), pltpu.roll(r, 1, 1))


def main_kernel(
    own_ref, blocks_ref, phi_hbm,
    arrived_hbm, pot_ref, table_ref,
    phi, phi_t, sbuf, rbuf_upper, rbuf_lower, lmat, scaled, pieces,
    asked, own_table, own_key, table_s, own_table_s, own_key_s,
    dens, near, source, field, coarse, corr, tz, ty, tx,
    phi_sem, local_sem, ask_send, ask_recv, out_send, out_recv, near_send, near_recv,
    tot_send, tot_recv, back_send, back_recv, self_sem,
):
    rbufs = (rbuf_upper, rbuf_lower)
    x, y, w, c = here()
    me = x * 32 + y * 8 + w * 2 + c

    phi_copy = pltpu.make_async_copy(phi_hbm, phi, phi_sem)
    phi_copy.start()

    axes = (
        [(0, 0, k // 2, k % 2) for k in range(1, 8)],
        [(0, k, 0, 0) for k in range(1, 4)],
        [(k, 0, 0, 0) for k in range(1, 4)],
    )
    barrier = pltpu.get_barrier_semaphore()

    @pl.loop(1, NDEV)
    def _(k):
        pl.semaphore_signal(barrier, inc=1, device_id=beyond(offset_of(k)), device_id_type=MESH)

    asked[0] = jnp.zeros((1, 128), jnp.int32)
    asked[0, :, 0:NPAIR] = own_ref[...]
    lane = lax.broadcasted_iota(jnp.int32, (NDEV, 1, 128), 2)
    own = asked[0:1]
    held = own >> 5
    key = (
        (((x - (held >> 5)) & 3) << 5)
        | (((y - (held >> 3)) & 3) << 3)
        | (((w - (held >> 1)) & 3) << 1)
        | ((c + held) & 1)
    )
    own_key[...] = key
    match = (key == lax.broadcasted_iota(jnp.int32, (NDEV, 1, 128), 0)) & (lane < NPAIR)
    first = jnp.min(jnp.where(match, lane, NPAIR - 1), axis=2, keepdims=True)
    last = jnp.max(jnp.where(match, lane, 0), axis=2, keepdims=True)
    own_table[...] = jnp.where(lane == 0, first, last)
    key_copy = pltpu.make_async_copy(own_key, own_key_s, local_sem.at[0])
    key_copy.start()
    own_copy = pltpu.make_async_copy(own_table, own_table_s, local_sem.at[1])
    own_copy.start()

    pl.semaphore_wait(barrier, NDEV - 1)

    for axis, (offsets, width) in enumerate(zip(axes, (1, 8, 32))):
        for offset in offsets:
            k = number(offset)
            remote(
                asked.at[pl.ds(0, width)], asked.at[pl.ds(k, width)],
                ask_send.at[axis], ask_recv.at[axis], before(offset),
            ).start()
        span = pl.ds(width, len(offsets) * width)
        remote(
            asked.at[span], asked.at[span], ask_send.at[axis], ask_recv.at[axis],
            before(offsets[0]),
        ).wait()

    wanted = asked[...]
    match = ((wanted >> 5) == me) & (lane < NPAIR)
    value = lane * 32 + (wanted & 31)
    first = jnp.min(jnp.where(match, value, 4096), axis=2, keepdims=True)
    last = jnp.max(jnp.where(match, value, -1), axis=2, keepdims=True)
    table = jnp.where(lane == 0, first & 31, last & 31)
    table = jnp.where(lane == 2, (last >= 0).astype(jnp.int32), table)
    table = jnp.where(lane == 3, (last > first).astype(jnp.int32), table)
    table_ref[...] = table
    table_copy = pltpu.make_async_copy(table_ref, table_s, local_sem.at[2])
    table_copy.start()
    table_copy.wait()

    for h in range(2):
        rows = pl.ds(h * HALF, HALF)

        @pl.loop(0, NDEV)
        def _(i):
            offset = turn(i)
            k = number(offset)
            sbuf[h, 2 * k] = blocks_ref[table_s[k, 0, 0], rows, :]
            sbuf[h, 2 * k + 1] = blocks_ref[table_s[k, 0, 1], rows, :]
            span = pl.ds(2 * k, 2)

            @pl.when(k != 0)
            def _():
                remote(
                    sbuf.at[h, span], rbufs[h].at[span], out_send.at[h], out_recv.at[h],
                    beyond(offset),
                ).start()

            @pl.when(k == 0)
            def _():
                rbufs[h][0] = sbuf[h, 0]
                rbufs[h][1] = sbuf[h, 1]

    phi_copy.wait()

    @pl.loop(0, NCHUNK)
    def _(j):
        cells = pl.ds(pl.multiple_of(j * CHUNK, CHUNK), CHUNK)
        for a in range(ORB_BLOCKS):
            phi_t[a * BLOCK:(a + 1) * BLOCK, cells] = phi[cells, a * BLOCK:(a + 1) * BLOCK].T

    key_copy.wait()
    own_copy.wait()
    others = pl.ds(2, NSLOT - 2)
    for h in range(2):
        remote(
            sbuf.at[h, others], rbufs[h].at[others], out_send.at[h], out_recv.at[h],
            beyond((0, 0, 0, 1)),
        ).wait()

        @pl.loop(0, ORB_BLOCKS)
        def _(a):
            rows = pl.ds(pl.multiple_of(a * HALF, HALF), HALF)
            for b in range(ORB_BLOCKS):
                p = a * ORB_BLOCKS + b
                k = own_key_s[0, 0, p]
                slot = 2 * k + (own_table_s[k, 0, 0] != p).astype(jnp.int32)
                lmat[rows, b * BLOCK:(b + 1) * BLOCK] = rbufs[h][slot]

        @pl.loop(0, NCHUNK)
        def _(j):
            cells = pl.ds(pl.multiple_of(j * CHUNK, CHUNK), CHUNK)
            product = jnp.dot(
                lmat[...], phi_t[:, cells], preferred_element_type=jnp.float32
            )
            total = jnp.zeros((HALF, CHUNK), jnp.float32)
            for a in range(ORB_BLOCKS):
                top = a * BLOCK + h * HALF
                total = total + product[a * HALF:(a + 1) * HALF] * phi_t[
                    top:top + HALF, cells
                ].astype(jnp.float32)
            line = jnp.sum(total, axis=0, keepdims=True)
            if h == 0:
                dens[pl.ds(j, 1), :] = line
            else:
                dens[pl.ds(j, 1), :] += line

    spots = [
        (bx, by, bz)
        for bx in range(3) for by in range(3) for bz in range(3)
        if (bx, by, bz) != (1, 1, 1)
    ]
    z = w * 2 + c
    for n, (bx, by, bz) in enumerate(spots):
        remote(
            dens, near.at[n], near_send, near_recv,
            ((x + 5 - bx) % 4, (y + 5 - by) % 4, (z + 9 - bz) % 8),
        ).start()

    tz[0] = jnp.broadcast_to(jnp.sum(dens[...], keepdims=True), (8, 128))

    def spread(axis, held_sums):
        for offset in axes[axis]:
            place = sum(offset) if axis else offset[2] * 2 + offset[3]
            remote(
                held_sums.at[0], held_sums.at[place], tot_send.at[axis], tot_recv.at[axis],
                before(offset),
            ).start()

    def gathered(axis, held_sums):
        span = pl.ds(1, len(axes[axis]))
        remote(
            held_sums.at[span], held_sums.at[span], tot_send.at[axis], tot_recv.at[axis],
            before(axes[axis][0]),
        ).wait()
        return jnp.sum(held_sums[...], axis=0)

    spread(0, tz)
    remote(near, near, near_send, near_recv, beyond((0, 0, 0, 1))).wait()
    source[1, 16:32, 256:512] = dens[...]
    for n, (bx, by, bz) in enumerate(spots):
        source[bz, bx * 16:bx * 16 + 16, by * 256:by * 256 + 256] = near[n]

    row48 = lax.broadcasted_iota(jnp.int32, (48, 768), 0)
    lane48 = lax.broadcasted_iota(jnp.int32, (48, 768), 1)
    zlane = lane48 % 16
    for b in range(3):
        field[b] = (OMEGA / FINE) * source[b]
    for _ in range(NPRE - 1):
        around = beside([field[b] for b in range(3)], 1, zlane)
        for b in range(3):
            field[b] = field[b] + OMEGA * (source[b] - (FINE * field[b] - around[b])) / FINE
    around = beside([field[b] for b in range(3)], 1, zlane)
    for b in range(3):
        rest = source[b] - (FINE * field[b] - around[b])
        coarse[b] = 0.5 * pair_sums(rest, row48, lane48)
        corr[b] = (OMEGA / COARSE) * coarse[b]
    ty[0] = gathered(0, tz)
    spread(1, ty)
    for _ in range(NCOARSE - 1):
        around = beside([corr[b] for b in range(3)], 2, zlane)
        for b in range(3):
            corr[b] = corr[b] + OMEGA * (coarse[b] - (COARSE * corr[b] - around[b])) / COARSE
    tx[0] = gathered(1, ty)
    spread(2, tx)
    for b in range(3):
        field[b] = field[b] + corr[b]
    for _ in range(NPOST):
        around = beside([field[b] for b in range(3)], 1, zlane)
        for b in range(3):
            field[b] = field[b] + OMEGA * (source[b] - (FINE * field[b] - around[b])) / FINE
    total = gathered(2, tx)
    mean = total[0:1, 0:1] * (1.0 / TOTAL_CELLS)
    pot_ref[...] = field[1, 16:32, 256:512] - constant_response() * mean

    for h in range(2):
        rows_in = [a * BLOCK + h * HALF for a in range(ORB_BLOCKS)]

        @pl.loop(0, NCHUNK)
        def _(j):
            cells = pl.ds(pl.multiple_of(j * CHUNK, CHUNK), CHUNK)
            line = pot_ref[pl.ds(j, 1), :]
            for a in range(ORB_BLOCKS):
                scaled[a * HALF:(a + 1) * HALF, cells] = (
                    phi_t[rows_in[a]:rows_in[a] + HALF, cells].astype(jnp.float32) * line
                ).astype(jnp.bfloat16)

        @pl.loop(0, ORB_BLOCKS // 2)
        def _(t):
            columns = pl.ds(pl.multiple_of(t * 2 * BLOCK, 2 * BLOCK), 2 * BLOCK)
            matrix = jnp.dot(
                scaled[...], phi[:, columns], preferred_element_type=jnp.float32
            ) * (CELLS ** -0.5)
            matrix = matrix.astype(jnp.bfloat16)
            for a in range(ORB_BLOCKS):
                for j in range(2):
                    pieces[a * ORB_BLOCKS + 2 * t + j] = matrix[
                        a * HALF:(a + 1) * HALF, j * BLOCK:(j + 1) * BLOCK
                    ]

        @pl.loop(0, NDEV)
        def _(i):
            offset = turn(i)
            k = number(offset)
            sbuf[h, 2 * k] = pieces[own_table_s[k, 0, 0]]
            sbuf[h, 2 * k + 1] = pieces[own_table_s[k, 0, 1]]
            span = pl.ds(2 * k, 2)

            @pl.when(k != 0)
            def _():
                remote(
                    sbuf.at[h, span], arrived_hbm.at[h, span], back_send.at[h], back_recv.at[h],
                    before(offset),
                ).start()

        pltpu.make_async_copy(
            sbuf.at[h, pl.ds(0, 2)], arrived_hbm.at[h, pl.ds(0, 2)], self_sem.at[h]
        ).start()

    for h in range(2):
        pltpu.make_async_copy(
            sbuf.at[h, pl.ds(0, 2)], arrived_hbm.at[h, pl.ds(0, 2)], self_sem.at[h]
        ).wait()
        remote(
            sbuf.at[h, others], arrived_hbm.at[h, others], back_send.at[h], back_recv.at[h],
            beyond((0, 0, 0, 1)),
        ).wait()


GROUP = 32


def add_kernel(table, arrived, out):
    step = pl.program_id(0)

    @pl.when(step == 0)
    def _():
        out[...] = jnp.zeros_like(out)

    @pl.loop(0, GROUP // 2)
    def _(i):
        k = step * (GROUP // 2) + i
        for s in range(2):
            @pl.when(table[k, 0, 2 + s] != 0)
            def _():
                place = table[k, 0, s]
                for h in range(2):
                    out[place, h * HALF:(h + 1) * HALF, :] += arrived[h, 2 * i + s].astype(
                        jnp.float32
                    )


def body(density_blocks, orbital_values, pair_index):
    phi = orbital_values.reshape(CELLS, LOCAL_ORB)
    vmem = pl.BlockSpec(memory_space=pltpu.VMEM)
    anywhere = pl.BlockSpec(memory_space=pl.ANY)
    dma = pltpu.SemaphoreType.DMA
    slots = (2, NSLOT, HALF, BLOCK)
    arrived, pot, table = pl.pallas_call(
        main_kernel,
        out_shape=(
            jax.ShapeDtypeStruct(slots, jnp.bfloat16),
            jax.ShapeDtypeStruct((16, 256), jnp.float32),
            jax.ShapeDtypeStruct((NDEV, 1, 128), jnp.int32),
        ),
        in_specs=[vmem, vmem, anywhere],
        out_specs=(anywhere, vmem, vmem),
        scratch_shapes=[
            pltpu.VMEM((CELLS, LOCAL_ORB), jnp.bfloat16),
            pltpu.VMEM((LOCAL_ORB, CELLS), jnp.bfloat16),
            pltpu.VMEM(slots, jnp.bfloat16),
            pltpu.VMEM(slots[1:], jnp.bfloat16),
            pltpu.VMEM(slots[1:], jnp.bfloat16),
            pltpu.VMEM((ORB_BLOCKS * HALF, LOCAL_ORB), jnp.bfloat16),
            pltpu.VMEM((ORB_BLOCKS * HALF, CELLS), jnp.bfloat16),
            pltpu.VMEM((NPAIR, HALF, BLOCK), jnp.bfloat16),
            pltpu.VMEM((NDEV, 1, 128), jnp.int32),
            pltpu.VMEM((NDEV, 1, 128), jnp.int32),
            pltpu.VMEM((1, 1, 128), jnp.int32),
            pltpu.SMEM((NDEV, 1, 128), jnp.int32),
            pltpu.SMEM((NDEV, 1, 128), jnp.int32),
            pltpu.SMEM((1, 1, 128), jnp.int32),
            pltpu.VMEM((16, 256), jnp.float32),
            pltpu.VMEM((26, 16, 256), jnp.float32),
            pltpu.VMEM((3, 48, 768), jnp.float32),
            pltpu.VMEM((3, 48, 768), jnp.float32),
            pltpu.VMEM((3, 48, 768), jnp.float32),
            pltpu.VMEM((3, 48, 768), jnp.float32),
            pltpu.VMEM((8, 8, 128), jnp.float32),
            pltpu.VMEM((4, 8, 128), jnp.float32),
            pltpu.VMEM((4, 8, 128), jnp.float32),
            dma, dma((3,)), dma((3,)), dma((3,)), dma((2,)), dma((2,)), dma, dma,
            dma((3,)), dma((3,)), dma((2,)), dma((2,)), dma((2,)),
        ],
        compiler_params=pltpu.CompilerParams(
            collective_id=0, has_side_effects=True, vmem_limit_bytes=60 * 2**20
        ),
        cost_estimate=pl.CostEstimate(
            flops=4 * CELLS * LOCAL_ORB * LOCAL_ORB, bytes_accessed=40 * 2**20, transcendentals=0
        ),
        name="collocate_solve_integrate",
    )(pair_index, density_blocks, phi)
    summed = pl.pallas_call(
        add_kernel,
        grid=(NSLOT // GROUP,),
        out_shape=jax.ShapeDtypeStruct((NNZ_DEV, BLOCK, BLOCK), jnp.float32),
        in_specs=[
            pl.BlockSpec(memory_space=pltpu.SMEM),
            pl.BlockSpec((2, GROUP, HALF, BLOCK), lambda i: (0, i, 0, 0)),
        ],
        out_specs=pl.BlockSpec((NNZ_DEV, BLOCK, BLOCK), lambda i: (0, 0, 0)),
        compiler_params=pltpu.CompilerParams(vmem_limit_bytes=32 * 2**20),
        name="add_arrived",
    )(table, arrived)
    return summed, pot.reshape(16, 16, 16)


def solution(mesh):
    return jax.shard_map(
        body,
        mesh=mesh,
        in_specs=(
            P(("gx", "gy", "gz"), None, None),
            P("gx", "gy", "gz", None),
            P(("gx", "gy", "gz"), None),
        ),
        out_specs=(P(("gx", "gy", "gz"), None, None), P("gx", "gy", "gz")),
        check_vma=False,
    )
```

```python
import functools

import jax
import jax.numpy as jnp
from jax import lax
from jax.experimental import pallas as pl
from jax.experimental.pallas import tpu as pltpu
from jax.sharding import PartitionSpec as P

MESH = pl.DeviceIdType.MESH
ORB_BLOCKS = 10
NPAIR = 100
BLOCK = 128
QUARTER = 32
NDEV = 128
NPLANE = 32
NSLOT = 256
NNZ_DEV = 32
CELLS = 4096
LOCAL_ORB = 1280
CHUNK = 256
NCHUNK = CELLS // CHUNK
TOTAL_CELLS = 524288
PARTS = ((0, (32, 16)), (48, (32, 16)), (96, (16, 16)))
ROUND_ROWS = (80, 48)

OMEGA = 0.6
SCREEN = 0.05
FINE = 6.0 + SCREEN
COARSE = 6.0 + 4.0 * SCREEN
NPRE = 2
NCOARSE = 4
NPOST = 2


def constant_response():
    field = 0.0
    for _ in range(NPRE):
        field = field + OMEGA * (1.0 - (FINE - 6.0) * field) / FINE
    rest = 4.0 * (1.0 - (FINE - 6.0) * field)
    correction = 0.0
    for _ in range(NCOARSE):
        correction = correction + OMEGA * (rest - (COARSE - 6.0) * correction) / COARSE
    field = field + correction
    for _ in range(NPOST):
        field = field + OMEGA * (1.0 - (FINE - 6.0) * field) / FINE
    return field


def here():
    z = lax.axis_index("gz")
    return lax.axis_index("gx"), lax.axis_index("gy"), z // 2, z % 2


def beyond(offset):
    x, y, w, c = here()
    dx, dy, dw, dc = offset
    return (x + dx) % 4, (y + dy) % 4, ((w + dw) % 4) * 2 + (c + dc) % 2


def before(offset):
    dx, dy, dw, dc = offset
    return beyond((4 - dx, 4 - dy, 4 - dw, dc))


def offset_of(k):
    return k // 32, (k // 8) % 4, (k // 2) % 4, k % 2


def turn(i):
    a, b, e, c = i % 4, (i // 4) % 4, (i // 16) % 4, (i // 64 + i) % 2
    return a, (a + b) % 4, (a + e) % 4, c


def plane_turn(axis, i):
    a, b, c = i % 4, (i // 4) % 4, (i // 16 + i) % 2
    u, v = ((a + b) % 4, a) if axis == 1 else (a, (a + b) % 4)
    return u * 8 + v * 2 + c


def plane_offset(axis, t):
    u, v, c = t // 8, (t // 2) % 4, t % 2
    return ((0, u, v, c), (u, 0, v, c), (u, v, 0, c))[axis]


def along(axis, j):
    return tuple(j if n == axis else 0 for n in range(3)) + (0,)


def number(offset):
    dx, dy, dw, dc = offset
    return dx * 32 + dy * 8 + dw * 2 + dc


def remote(src, dst, send, recv, device):
    return pltpu.make_async_remote_copy(
        src_ref=src, dst_ref=dst, send_sem=send, recv_sem=recv,
        device_id=device, device_id_type=MESH,
    )


def beside(v, n):
    rows, lanes = v[0].shape
    zlane = lax.broadcasted_iota(jnp.int32, (rows, lanes), 1) % 16
    result = []
    for b in range(3):
        total = pltpu.roll(v[b], n, 0) + pltpu.roll(v[b], rows - n, 0)
        total = total + pltpu.roll(v[b], 16 * n, 1) + pltpu.roll(v[b], lanes - 16 * n, 1)
        up = jnp.where(
            zlane >= 16 - n,
            pltpu.roll(v[(b + 1) % 3], 16 - n, 1),
            pltpu.roll(v[b], lanes - n, 1),
        )
        down = jnp.where(
            zlane < n,
            pltpu.roll(v[(b + 2) % 3], lanes - 16 + n, 1),
            pltpu.roll(v[b], n, 1),
        )
        result.append(total + up + down)
    return result


def pair_sums(r):
    rows, lanes = r.shape
    row = lax.broadcasted_iota(jnp.int32, r.shape, 0)
    lane = lax.broadcasted_iota(jnp.int32, r.shape, 1)
    r = r + jnp.where(row % 2 == 0, pltpu.roll(r, rows - 1, 0), pltpu.roll(r, 1, 0))
    r = r + jnp.where(
        (lane // 16) % 2 == 0, pltpu.roll(r, lanes - 16, 1), pltpu.roll(r, 16, 1)
    )
    return r + jnp.where(lane % 2 == 0, pltpu.roll(r, lanes - 1, 1), pltpu.roll(r, 1, 1))


def first_last(match, value, low, high):
    first = jnp.min(jnp.where(match, value, high), axis=1, keepdims=True)
    last = jnp.max(jnp.where(match, value, low), axis=1, keepdims=True)
    return first, last


def main_kernel(
    own_ref, blocks_ref, phi_hbm,
    arrived_hbm, pot_ref, table_ref,
    phi, phi_t,
    ag_a, ag_b, ag_c,
    s0a, s0b, s0c, s1a, s1b, s1c,
    r0a, r0b, r0c, r1a, r1b, r1c,
    lmat0, lmat1, scaled, pieces,
    asked, own_table, own_key, send_table, own_table_s, own_key_s, send_table_s, place_s,
    dens, near, source, pre, field, coarse, corr, tz, ty, tx,
    phi_sem, local_sem, ask_send, ask_recv, ag_send, ag_recv, out_send, out_recv,
    near_send, near_recv, tot_send, tot_recv, back_send, back_recv, self_sem,
):
    gathered_blocks = (ag_a, ag_b, ag_c)
    sbufs = ((s0a, s0b, s0c), (s1a, s1b, s1c))
    rbufs = ((r0a, r0b, r0c), (r1a, r1b, r1c))
    lmats = (lmat0, lmat1)
    x, y, w, c = here()
    me = x * 32 + y * 8 + w * 2 + c

    phi_copy = pltpu.make_async_copy(phi_hbm, phi, phi_sem)
    phi_copy.start()

    axes = (
        [(0, 0, k // 2, k % 2) for k in range(1, 8)],
        [(0, k, 0, 0) for k in range(1, 4)],
        [(k, 0, 0, 0) for k in range(1, 4)],
    )
    barrier = pltpu.get_barrier_semaphore()
    for offsets in axes:
        for offset in offsets:
            pl.semaphore_signal(barrier, inc=1, device_id=beyond(offset), device_id_type=MESH)

    asked[0] = jnp.zeros((1, 128), jnp.int32)
    asked[0, :, 0:NPAIR] = own_ref[...]
    lane = lax.broadcasted_iota(jnp.int32, (NDEV, 128), 1)
    row = lax.broadcasted_iota(jnp.int32, (NDEV, 128), 0)
    own = asked[0]
    held = own >> 5
    key = (
        (((x - (held >> 5)) & 3) << 5)
        | (((y - (held >> 3)) & 3) << 3)
        | (((w - (held >> 1)) & 3) << 1)
        | ((c + held) & 1)
    )
    own_key[...] = key
    first, last = first_last((key == row) & (lane < NPAIR), lane, 0, NPAIR - 1)
    own_table[...] = jnp.where(lane == 0, first, last)
    key_copy = pltpu.make_async_copy(own_key, own_key_s, local_sem.at[0])
    key_copy.start()
    own_copy = pltpu.make_async_copy(own_table, own_table_s, local_sem.at[1])
    own_copy.start()
    for axis, (top, rounds) in enumerate(PARTS):
        gathered_blocks[axis][0:NNZ_DEV] = blocks_ref[:, top:top + sum(rounds), :]

    pl.semaphore_wait(barrier, 13)

    for axis, (offsets, width) in enumerate(zip(axes, (1, 8, 32))):
        for offset in offsets:
            k = number(offset)
            remote(
                asked.at[pl.ds(0, width)], asked.at[pl.ds(k, width)],
                ask_send.at[axis], ask_recv.at[axis], before(offset),
            ).start()
        if axis == 0:
            for j in (1, 3, 2):
                for part, (top, rounds) in enumerate(PARTS):
                    remote(
                        blocks_ref.at[:, pl.ds(top, sum(rounds)), :],
                        gathered_blocks[part].at[pl.ds(j * NNZ_DEV, NNZ_DEV)],
                        ag_send.at[part], ag_recv.at[part], before(along(part, j)),
                    ).start()
        span = pl.ds(width, len(offsets) * width)
        remote(
            asked.at[span], asked.at[span], ask_send.at[axis], ask_recv.at[axis],
            before(offsets[0]),
        ).wait()

    wanted = asked[:, 0, :]
    asks = (
        wanted[0:32],
        jnp.concatenate([wanted[n * 32:n * 32 + 8] for n in range(4)], axis=0),
        wanted,
    )
    for axis, base in enumerate((0, 32, 64)):
        ask = asks[axis]
        count = ask.shape[0]
        lane_n = lane[0:count]
        value = lane_n * 32 + (ask & 31)
        table = jnp.zeros((count, 128), jnp.int32)
        for j in range(4):
            holder = (
                ((x + j) % 4) * 32 + y * 8 + w * 2 + c,
                x * 32 + ((y + j) % 4) * 8 + w * 2 + c,
                x * 32 + y * 8 + ((w + j) % 4) * 2 + c,
            )[axis]
            first, last = first_last(
                ((ask >> 5) == holder) & (lane_n < NPAIR), value, 0, NNZ_DEV * 128 - 1
            )
            table = jnp.where(lane_n == 2 * j, j * NNZ_DEV + (first & 31), table)
            table = jnp.where(lane_n == 2 * j + 1, j * NNZ_DEV + (last & 31), table)
        send_table[base:base + count] = table
    table_copy = pltpu.make_async_copy(send_table, send_table_s, local_sem.at[2])
    table_copy.start()
    table_copy.wait()
    for part in range(3):
        span = pl.ds(NNZ_DEV, 3 * NNZ_DEV)
        remote(
            gathered_blocks[part].at[span], gathered_blocks[part].at[span],
            ag_send.at[part], ag_recv.at[part], before(along(part, 1)),
        ).wait()

    for r in range(2):
        @pl.loop(0, NPLANE)
        def _(i):
            for part, (top, rounds) in enumerate(PARTS):
                t = plane_turn(part, i)
                rows = pl.ds(sum(rounds[:r]), rounds[r])
                line = (t, 32 + t, 64 + (t // 8) * 32 + ((t // 2) % 4) * 8 + t % 2)[part]
                send, recv = sbufs[r][part], rbufs[r][part]
                for n in range(8):
                    send[8 * t + n] = gathered_blocks[part][send_table_s[line, n], rows, :]
                span = pl.ds(8 * t, 8)

                @pl.when(t != 0)
                def _():
                    remote(
                        send.at[span], recv.at[span], out_send.at[r, part], out_recv.at[r, part],
                        beyond(plane_offset(part, t)),
                    ).start()

                @pl.when(t == 0)
                def _():
                    for n in range(8):
                        recv[n] = send[n]

    key_copy.wait()
    own_copy.wait()

    @pl.loop(0, NPAIR)
    def _(p):
        k = own_key_s[0, p]
        rank = (own_table_s[k, 0] != p).astype(jnp.int32)
        dx, dy, dw = k >> 5, (k >> 3) & 3, (k >> 1) & 3
        place_s[0, p] = (k & 31) * 8 + ((4 - dx) & 3) * 2 + rank
        place_s[1, p] = (dx * 8 + (k & 7)) * 8 + ((4 - dy) & 3) * 2 + rank
        place_s[2, p] = (dx * 8 + dy * 2 + (k & 1)) * 8 + ((4 - dw) & 3) * 2 + rank

    first, last = first_last(
        ((wanted >> 5) == me) & (lane < NPAIR), lane * 32 + (wanted & 31), -1, NNZ_DEV * 128
    )
    table = jnp.where(lane == 0, first & 31, last & 31)
    table = jnp.where(lane == 2, (last >= 0).astype(jnp.int32), table)
    table = jnp.where(lane == 3, (last > first).astype(jnp.int32), table)
    table_ref[...] = table

    phi_copy.wait()

    @pl.loop(0, NCHUNK)
    def _(j):
        cells = pl.ds(pl.multiple_of(j * CHUNK, CHUNK), CHUNK)
        for a in range(ORB_BLOCKS):
            phi_t[a * BLOCK:(a + 1) * BLOCK, cells] = phi[cells, a * BLOCK:(a + 1) * BLOCK].T

    spots = [
        (bx, by, bz)
        for bx in range(3) for by in range(3) for bz in range(3)
        if (bx, by, bz) != (1, 1, 1)
    ]
    z = w * 2 + c

    def send_density(part):
        for n, (bx, by, bz) in enumerate(spots):
            remote(
                dens.at[pl.ds(8 * part, 8)], near.at[part, n],
                near_send.at[part], near_recv.at[part],
                ((x + 5 - bx) % 4, (y + 5 - by) % 4, (z + 9 - bz) % 8),
            ).start()

    for r in range(2):
        for part in range(3):
            others = pl.ds(8, NSLOT - 8)
            remote(
                sbufs[r][part].at[others], rbufs[r][part].at[others],
                out_send.at[r, part], out_recv.at[r, part], beyond(along(2, 1)),
            ).wait()

        @pl.loop(0, ORB_BLOCKS)
        def _(a):
            for b in range(ORB_BLOCKS):
                into = 0
                for part, (top, rounds) in enumerate(PARTS):
                    rows = pl.ds(pl.multiple_of(a * ROUND_ROWS[r] + into, 16), rounds[r])
                    lmats[r][rows, b * BLOCK:(b + 1) * BLOCK] = rbufs[r][part][
                        place_s[part, a * ORB_BLOCKS + b]
                    ]
                    into += rounds[r]

        def collocate(j):
            cells = pl.ds(pl.multiple_of(j * CHUNK, CHUNK), CHUNK)
            product = jnp.dot(
                lmats[r][...], phi_t[:, cells], preferred_element_type=jnp.float32
            )
            total = jnp.zeros((16, CHUNK), jnp.float32)
            for a in range(ORB_BLOCKS):
                into = a * ROUND_ROWS[r]
                for part, (top, rounds) in enumerate(PARTS):
                    start = a * BLOCK + top + sum(rounds[:r])
                    for n in range(0, rounds[r], 16):
                        total = total + product[into + n:into + n + 16] * phi_t[
                            start + n:start + n + 16, cells
                        ].astype(jnp.float32)
                    into += rounds[r]
            line = jnp.sum(total, axis=0, keepdims=True)
            if r == 0:
                dens[pl.ds(j, 1), :] = line
            else:
                dens[pl.ds(j, 1), :] += line

        if r == 0:
            pl.loop(0, NCHUNK)(collocate)
        else:
            pl.loop(0, NCHUNK // 2)(collocate)
            send_density(0)
            pl.loop(NCHUNK // 2, NCHUNK)(collocate)
            send_density(1)

    tz[0] = jnp.broadcast_to(jnp.sum(dens[...], keepdims=True), (8, 128))

    def spread(axis, held_sums):
        for offset in axes[axis]:
            place = sum(offset) if axis else offset[2] * 2 + offset[3]
            remote(
                held_sums.at[0], held_sums.at[place], tot_send.at[axis], tot_recv.at[axis],
                before(offset),
            ).start()

    def gathered(axis, held_sums):
        span = pl.ds(1, len(axes[axis]))
        remote(
            held_sums.at[span], held_sums.at[span], tot_send.at[axis], tot_recv.at[axis],
            before(axes[axis][0]),
        ).wait()
        return jnp.sum(held_sums[...], axis=0)

    spread(0, tz)
    source[1, 16:32, 256:512] = dens[...]
    for part in range(2):
        remote(
            near.at[part], near.at[part], near_send.at[part], near_recv.at[part],
            beyond((0, 0, 0, 1)),
        ).wait()
        for n, (bx, by, bz) in enumerate(spots):
            top = bx * 16 + part * 8
            source[bz, top:top + 8, by * 256:by * 256 + 256] = near[part, n]

    inner = (slice(8, 40), slice(128, 640))
    slabs = range(3)
    gain, keep = OMEGA / FINE, 1.0 - OMEGA
    wide = [source[b] for b in slabs]
    around = beside([gain * v for v in wide], 1)
    for b in slabs:
        pre[b] = (keep * gain + gain) * wide[b] + gain * around[b]
    wide = [pre[b] for b in slabs]
    around = beside(wide, 1)
    for b in slabs:
        rest = source[(b,) + inner] - FINE * wide[b][inner] + around[b][inner]
        coarse[b] = (0.5 * OMEGA / COARSE) * pair_sums(rest)
        corr[b] = coarse[b]
    ty[0] = gathered(0, tz)
    spread(1, ty)
    for _ in range(NCOARSE - 1):
        around = beside([corr[b] for b in slabs], 2)
        for b in slabs:
            corr[b] = keep * corr[b] + coarse[b] + (OMEGA / COARSE) * around[b]
    tx[0] = gathered(1, ty)
    spread(2, tx)
    for b in slabs:
        field[b] = pre[(b,) + inner] + corr[b]
    for _ in range(NPOST):
        around = beside([field[b] for b in slabs], 1)
        for b in slabs:
            field[b] = keep * field[b] + gain * (source[(b,) + inner] + around[b])
    total = gathered(2, tx)
    mean = total[0:1, 0:1] * (1.0 / TOTAL_CELLS)
    pot_ref[...] = field[1, 8:24, 128:384] - constant_response() * mean

    returning = (s0a, s0b, r0a, r0b)
    for q, send in enumerate(returning):
        rows_in = [a * BLOCK + q * QUARTER for a in range(ORB_BLOCKS)]

        @pl.loop(0, NCHUNK)
        def _(j):
            cells = pl.ds(pl.multiple_of(j * CHUNK, CHUNK), CHUNK)
            line = pot_ref[pl.ds(j, 1), :]
            for a in range(ORB_BLOCKS):
                scaled[a * QUARTER:(a + 1) * QUARTER, cells] = (
                    phi_t[rows_in[a]:rows_in[a] + QUARTER, cells].astype(jnp.float32) * line
                ).astype(jnp.bfloat16)

        @pl.loop(0, ORB_BLOCKS // 2)
        def _(t):
            columns = pl.ds(pl.multiple_of(t * 2 * BLOCK, 2 * BLOCK), 2 * BLOCK)
            matrix = jnp.dot(
                scaled[...], phi[:, columns], preferred_element_type=jnp.float32
            ) * (CELLS ** -0.5)
            matrix = matrix.astype(jnp.bfloat16)
            for a in range(ORB_BLOCKS):
                for j in range(2):
                    pieces[a * ORB_BLOCKS + 2 * t + j] = matrix[
                        a * QUARTER:(a + 1) * QUARTER, j * BLOCK:(j + 1) * BLOCK
                    ]

        @pl.loop(0, NDEV)
        def _(i):
            offset = turn(i)
            k = number(offset)
            send[2 * k] = pieces[own_table_s[k, 0]]
            send[2 * k + 1] = pieces[own_table_s[k, 1]]
            span = pl.ds(2 * k, 2)

            @pl.when(k != 0)
            def _():
                remote(
                    send.at[span], arrived_hbm.at[q, span], back_send.at[q], back_recv.at[q],
                    before(offset),
                ).start()

        pltpu.make_async_copy(
            send.at[pl.ds(0, 2)], arrived_hbm.at[q, pl.ds(0, 2)], self_sem.at[q]
        ).start()

    for q, send in enumerate(returning):
        pltpu.make_async_copy(
            send.at[pl.ds(0, 2)], arrived_hbm.at[q, pl.ds(0, 2)], self_sem.at[q]
        ).wait()
        others = pl.ds(2, NSLOT - 2)
        remote(
            send.at[others], arrived_hbm.at[q, others], back_send.at[q], back_recv.at[q],
            beyond((0, 0, 0, 1)),
        ).wait()


def add_kernel(table, arrived, out, buf, sems):
    def fetch(k):
        span = pl.ds(2 * k, 2)
        return pltpu.make_async_copy(arrived.at[:, span], buf.at[:, span], sems.at[k])

    @pl.loop(0, NDEV)
    def _(k):
        @pl.when(table[k, 2] != 0)
        def _():
            fetch(k).start()

    out[...] = jnp.zeros_like(out)

    @pl.loop(0, NDEV)
    def _(k):
        @pl.when(table[k, 2] != 0)
        def _():
            fetch(k).wait()
        for s in range(2):
            @pl.when(table[k, 2 + s] != 0)
            def _():
                place = table[k, s]
                for q in range(4):
                    out[place, q * QUARTER:(q + 1) * QUARTER, :] += buf[q, 2 * k + s].astype(
                        jnp.float32
                    )


def body(density_blocks, orbital_values, pair_index):
    phi = orbital_values.reshape(CELLS, LOCAL_ORB)
    vmem = pl.BlockSpec(memory_space=pltpu.VMEM)
    smem = pl.BlockSpec(memory_space=pltpu.SMEM)
    anywhere = pl.BlockSpec(memory_space=pl.ANY)
    dma = pltpu.SemaphoreType.DMA
    slots = (4, NSLOT, QUARTER, BLOCK)
    bf16, f32, i32 = jnp.bfloat16, jnp.float32, jnp.int32
    transit = [
        pltpu.VMEM((NSLOT, rounds[r], BLOCK), bf16) for r in range(2) for top, rounds in PARTS
    ]
    arrived, pot, table = pl.pallas_call(
        main_kernel,
        out_shape=(
            jax.ShapeDtypeStruct(slots, bf16),
            jax.ShapeDtypeStruct((16, 256), f32),
            jax.ShapeDtypeStruct((NDEV, 128), i32),
        ),
        in_specs=[vmem, vmem, anywhere],
        out_specs=(anywhere, vmem, vmem),
        scratch_shapes=[
            pltpu.VMEM((CELLS, LOCAL_ORB), bf16),
            pltpu.VMEM((LOCAL_ORB, CELLS), bf16),
        ] + [
            pltpu.VMEM((4 * NNZ_DEV, sum(rounds), BLOCK), bf16) for top, rounds in PARTS
        ] + transit + transit + [
            pltpu.VMEM((ORB_BLOCKS * ROUND_ROWS[0], LOCAL_ORB), bf16),
            pltpu.VMEM((ORB_BLOCKS * ROUND_ROWS[1], LOCAL_ORB), bf16),
            pltpu.VMEM((ORB_BLOCKS * QUARTER, CELLS), bf16),
            pltpu.VMEM((NPAIR, QUARTER, BLOCK), bf16),
            pltpu.VMEM((NDEV, 1, 128), i32),
            pltpu.VMEM((NDEV, 128), i32),
            pltpu.VMEM((1, 128), i32),
            pltpu.VMEM((192, 128), i32),
            pltpu.SMEM((NDEV, 128), i32),
            pltpu.SMEM((1, 128), i32),
            pltpu.SMEM((192, 128), i32),
            pltpu.SMEM((3, 128), i32),
            pltpu.VMEM((16, 256), f32),
            pltpu.VMEM((2, 26, 8, 256), f32),
            pltpu.VMEM((3, 48, 768), f32),
            pltpu.VMEM((3, 48, 768), f32),
            pltpu.VMEM((3, 32, 512), f32),
            pltpu.VMEM((3, 32, 512), f32),
            pltpu.VMEM((3, 32, 512), f32),
            pltpu.VMEM((8, 8, 128), f32),
            pltpu.VMEM((4, 8, 128), f32),
            pltpu.VMEM((4, 8, 128), f32),
            dma, dma((3,)), dma((3,)), dma((3,)), dma((3,)), dma((3,)), dma((2, 3)), dma((2, 3)),
            dma((2,)), dma((2,)), dma((3,)), dma((3,)), dma((4,)), dma((4,)), dma((4,)),
        ],
        compiler_params=pltpu.CompilerParams(
            collective_id=0, has_side_effects=True, vmem_limit_bytes=60 * 2**20
        ),
        cost_estimate=pl.CostEstimate(
            flops=4 * CELLS * LOCAL_ORB * LOCAL_ORB, bytes_accessed=40 * 2**20, transcendentals=0
        ),
        name="collocate_solve_integrate",
    )(pair_index, density_blocks, phi)
    summed = pl.pallas_call(
        add_kernel,
        out_shape=jax.ShapeDtypeStruct((NNZ_DEV, BLOCK, BLOCK), f32),
        in_specs=[smem, anywhere],
        out_specs=vmem,
        scratch_shapes=[pltpu.VMEM(slots, bf16), dma((NDEV,))],
        compiler_params=pltpu.CompilerParams(vmem_limit_bytes=60 * 2**20),
        name="add_arrived",
    )(table, arrived)
    return summed, pot.reshape(16, 16, 16)


def solution(mesh):
    return jax.shard_map(
        body,
        mesh=mesh,
        in_specs=(
            P(("gx", "gy", "gz"), None, None),
            P("gx", "gy", "gz", None),
            P(("gx", "gy", "gz"), None),
        ),
        out_specs=(P(("gx", "gy", "gz"), None, None), P("gx", "gy", "gz")),
        check_vma=False,
    )
```

```python
import functools

import jax
import jax.numpy as jnp
from jax import lax
from jax.experimental import pallas as pl
from jax.experimental.pallas import tpu as pltpu
from jax.sharding import PartitionSpec as P

MESH = pl.DeviceIdType.MESH
ORB_BLOCKS = 10
NPAIR = 100
BLOCK = 128
QUARTER = 32
NDEV = 128
NPLANE = 32
NSLOT = 256
NNZ_DEV = 32
CELLS = 4096
LOCAL_ORB = 1280
CHUNK = 256
NCHUNK = CELLS // CHUNK
TOTAL_CELLS = 524288
GROUP = 16
PARTS = ((0, 16, 32), (48, 64, 80), (96, 112, 32))
ROUND_TOPS = ((0, 16, 48, 64, 96, 112), (32, 80))

OMEGA = 0.6
SCREEN = 0.05
FINE = 6.0 + SCREEN
COARSE = 6.0 + 4.0 * SCREEN
NPRE = 2
NCOARSE = 4
NPOST = 2


def constant_response():
    field = 0.0
    for _ in range(NPRE):
        field = field + OMEGA * (1.0 - (FINE - 6.0) * field) / FINE
    rest = 4.0 * (1.0 - (FINE - 6.0) * field)
    correction = 0.0
    for _ in range(NCOARSE):
        correction = correction + OMEGA * (rest - (COARSE - 6.0) * correction) / COARSE
    field = field + correction
    for _ in range(NPOST):
        field = field + OMEGA * (1.0 - (FINE - 6.0) * field) / FINE
    return field


def here():
    z = lax.axis_index("gz")
    return lax.axis_index("gx"), lax.axis_index("gy"), z // 2, z % 2


def beyond(offset):
    x, y, w, c = here()
    dx, dy, dw, dc = offset
    return (x + dx) % 4, (y + dy) % 4, ((w + dw) % 4) * 2 + (c + dc) % 2


def before(offset):
    dx, dy, dw, dc = offset
    return beyond((4 - dx, 4 - dy, 4 - dw, dc))


def offset_of(k):
    return k // 32, (k // 8) % 4, (k // 2) % 4, k % 2


def turn(i):
    a, b, e, c = i % 4, (i // 4) % 4, (i // 16) % 4, (i // 64 + i) % 2
    return a, (a + b) % 4, (a + e) % 4, c


def plane_turn(axis, i):
    a, b, c = i % 4, (i // 4) % 4, (i // 16 + i) % 2
    u, v = ((a + b) % 4, a) if axis == 1 else (a, (a + b) % 4)
    return u * 8 + v * 2 + c


def plane_offset(axis, t):
    u, v, c = t // 8, (t // 2) % 4, t % 2
    return ((0, u, v, c), (u, 0, v, c), (u, v, 0, c))[axis]


def along(axis, j):
    return tuple(j if n == axis else 0 for n in range(3)) + (0,)


def number(offset):
    dx, dy, dw, dc = offset
    return dx * 32 + dy * 8 + dw * 2 + dc


def remote(src, dst, send, recv, device):
    return pltpu.make_async_remote_copy(
        src_ref=src, dst_ref=dst, send_sem=send, recv_sem=recv,
        device_id=device, device_id_type=MESH,
    )


def beside(v, n):
    rows, lanes = v[0].shape
    zlane = lax.broadcasted_iota(jnp.int32, (rows, lanes), 1) % 16
    result = []
    for b in range(3):
        total = pltpu.roll(v[b], n, 0) + pltpu.roll(v[b], rows - n, 0)
        total = total + pltpu.roll(v[b], 16 * n, 1) + pltpu.roll(v[b], lanes - 16 * n, 1)
        up = jnp.where(
            zlane >= 16 - n,
            pltpu.roll(v[(b + 1) % 3], 16 - n, 1),
            pltpu.roll(v[b], lanes - n, 1),
        )
        down = jnp.where(
            zlane < n,
            pltpu.roll(v[(b + 2) % 3], lanes - 16 + n, 1),
            pltpu.roll(v[b], n, 1),
        )
        result.append(total + up + down)
    return result


def pair_sums(r):
    rows, lanes = r.shape
    row = lax.broadcasted_iota(jnp.int32, r.shape, 0)
    lane = lax.broadcasted_iota(jnp.int32, r.shape, 1)
    r = r + jnp.where(row % 2 == 0, pltpu.roll(r, rows - 1, 0), pltpu.roll(r, 1, 0))
    r = r + jnp.where(
        (lane // 16) % 2 == 0, pltpu.roll(r, lanes - 16, 1), pltpu.roll(r, 16, 1)
    )
    return r + jnp.where(lane % 2 == 0, pltpu.roll(r, lanes - 1, 1), pltpu.roll(r, 1, 1))


def first_last(match, value, low, high):
    first = jnp.min(jnp.where(match, value, high), axis=1, keepdims=True)
    last = jnp.max(jnp.where(match, value, low), axis=1, keepdims=True)
    return first, last


def main_kernel(
    own_ref, blocks_ref, phi_hbm,
    out_ref, pot_ref,
    phi, phi_t,
    ag_a, ag_b, ag_c,
    s0a, s0b, s0c, s1,
    r0a, r0b, r0c, r1,
    lmat0, lmat1, scaled, pieces, sums,
    asked, own_table, own_key, send_table, order,
    own_table_s, own_key_s, send_table_s, place_s, order_s,
    dens, near, source, pre, field, coarse, corr, tz, ty, tx,
    phi_sem, local_sem, ask_send, ask_recv, ag_send, ag_recv, out_send, out_recv,
    near_send, near_recv, tot_send, tot_recv, back_send, back_recv,
):
    gathered_blocks = (ag_a, ag_b, ag_c)
    sbufs, rbufs = (s0a, s0b, s0c, s1), (r0a, r0b, r0c, r1)
    lmats = (lmat0, lmat1)
    x, y, w, c = here()
    me = x * 32 + y * 8 + w * 2 + c

    phi_copy = pltpu.make_async_copy(phi_hbm, phi, phi_sem)
    phi_copy.start()

    axes = (
        [(0, 0, k // 2, k % 2) for k in range(1, 8)],
        [(0, k, 0, 0) for k in range(1, 4)],
        [(k, 0, 0, 0) for k in range(1, 4)],
    )
    barrier = pltpu.get_barrier_semaphore()
    for offsets in axes:
        for offset in offsets:
            pl.semaphore_signal(barrier, inc=1, device_id=beyond(offset), device_id_type=MESH)

    asked[0] = jnp.zeros((1, 128), jnp.int32)
    asked[0, :, 0:NPAIR] = own_ref[...]
    lane = lax.broadcasted_iota(jnp.int32, (NDEV, 128), 1)
    row = lax.broadcasted_iota(jnp.int32, (NDEV, 128), 0)
    own = asked[0]
    held = own >> 5
    key = (
        (((x - (held >> 5)) & 3) << 5)
        | (((y - (held >> 3)) & 3) << 3)
        | (((w - (held >> 1)) & 3) << 1)
        | ((c + held) & 1)
    )
    own_key[...] = key
    first, last = first_last((key == row) & (lane < NPAIR), lane, 0, NPAIR - 1)
    own_table[...] = jnp.where(lane == 0, first, last)
    key_copy = pltpu.make_async_copy(own_key, own_key_s, local_sem.at[0])
    key_copy.start()
    own_copy = pltpu.make_async_copy(own_table, own_table_s, local_sem.at[1])
    own_copy.start()
    for part, tops in enumerate(PARTS):
        for n, top in enumerate(tops):
            gathered_blocks[part][n, 0:NNZ_DEV] = blocks_ref[:, top:top + GROUP, :]

    pl.semaphore_wait(barrier, 13)

    for axis, (offsets, width) in enumerate(zip(axes, (1, 8, 32))):
        for offset in offsets:
            k = number(offset)
            remote(
                asked.at[pl.ds(0, width)], asked.at[pl.ds(k, width)],
                ask_send.at[axis], ask_recv.at[axis], before(offset),
            ).start()
        for j in (1, 3, 2):
            for part, tops in enumerate(PARTS):
                remote(
                    blocks_ref.at[:, pl.ds(tops[axis], GROUP), :],
                    gathered_blocks[part].at[axis, pl.ds(j * NNZ_DEV, NNZ_DEV)],
                    ag_send.at[part], ag_recv.at[part], before(along(part, j)),
                ).start()
        span = pl.ds(width, len(offsets) * width)
        remote(
            asked.at[span], asked.at[span], ask_send.at[axis], ask_recv.at[axis],
            before(offsets[0]),
        ).wait()

    wanted = asked[:, 0, :]
    asks = (
        wanted[0:32],
        jnp.concatenate([wanted[n * 32:n * 32 + 8] for n in range(4)], axis=0),
        wanted,
    )
    for axis, base in enumerate((0, 32, 64)):
        ask = asks[axis]
        count = ask.shape[0]
        lane_n = lane[0:count]
        value = lane_n * 32 + (ask & 31)
        table = jnp.zeros((count, 128), jnp.int32)
        for j in range(4):
            holder = (
                ((x + j) % 4) * 32 + y * 8 + w * 2 + c,
                x * 32 + ((y + j) % 4) * 8 + w * 2 + c,
                x * 32 + y * 8 + ((w + j) % 4) * 2 + c,
            )[axis]
            first, last = first_last(
                ((ask >> 5) == holder) & (lane_n < NPAIR), value, 0, NNZ_DEV * 128 - 1
            )
            table = jnp.where(lane_n == 2 * j, j * NNZ_DEV + (first & 31), table)
            table = jnp.where(lane_n == 2 * j + 1, j * NNZ_DEV + (last & 31), table)
        send_table[base:base + count] = table
    table_copy = pltpu.make_async_copy(send_table, send_table_s, local_sem.at[2])
    table_copy.start()
    table_copy.wait()
    for part in range(3):
        span = pl.ds(NNZ_DEV, 3 * NNZ_DEV)
        remote(
            gathered_blocks[part].at[:, span], gathered_blocks[part].at[:, span],
            ag_send.at[part], ag_recv.at[part], before(along(part, 1)),
        ).wait()

    def send_round(r):
        @pl.loop(0, NPLANE)
        def _(i):
            for part in range(3):
                t = plane_turn(part, i)
                line = (t, 32 + t, 64 + (t // 8) * 32 + ((t // 2) % 4) * 8 + t % 2)[part]
                if r == 0:
                    send, recv, base, count = sbufs[part], rbufs[part], 8 * t, 8
                    for n in range(8):
                        block = send_table_s[line, n]
                        for g in range(2):
                            send[base + n, g * GROUP:(g + 1) * GROUP] = gathered_blocks[part][g, block]
                else:
                    send, recv = s1, r1
                    base = (4 * t, 128 + 8 * t, 384 + 4 * t)[part]
                    slots = ((0, 2, 4, 6), range(8), (1, 3, 5, 7))[part]
                    count = len(slots)
                    for n, slot in enumerate(slots):
                        send[base + n] = gathered_blocks[part][2, send_table_s[line, slot]]
                span = pl.ds(base, count)

                @pl.when(t != 0)
                def _():
                    remote(
                        send.at[span], recv.at[span], out_send.at[r, part], out_recv.at[r, part],
                        beyond(plane_offset(part, t)),
                    ).start()

                @pl.when(t == 0)
                def _():
                    for n in range(count):
                        recv[base + n] = send[base + n]

    send_round(0)
    send_round(1)

    key_copy.wait()
    own_copy.wait()

    @pl.loop(0, NPAIR)
    def _(p):
        k = own_key_s[0, p]
        rank = (own_table_s[k, 0] != p).astype(jnp.int32)
        dx, dy, dw = k >> 5, (k >> 3) & 3, (k >> 1) & 3
        place_s[0, p] = (k & 31) * 8 + ((4 - dx) & 3) * 2 + rank
        place_s[1, p] = (dx * 8 + (k & 7)) * 8 + ((4 - dy) & 3) * 2 + rank
        place_s[2, p] = (dx * 8 + dy * 2 + (k & 1)) * 8 + ((4 - dw) & 3) * 2 + rank
        place_s[3, p] = rank

    first, last = first_last(
        ((wanted >> 5) == me) & (lane < NPAIR), lane * 32 + (wanted & 31), -1, NNZ_DEV * 128
    )
    blocks = [
        jnp.where(last >= 0, first & 31, NNZ_DEV), jnp.where(last > first, last & 31, NNZ_DEV)
    ]
    slots = [2 * row[:, 0:1], 2 * row[:, 0:1] + 1]
    keys = [block * NSLOT + slot for block, slot in zip(blocks, slots)]
    across = [jnp.broadcast_to(key, (NDEV, 128)).T for key in keys]
    ranks = [
        sum(jnp.sum((other < key).astype(jnp.int32), axis=1, keepdims=True) for other in across)
        for key in keys
    ]
    for n in range(2):
        at = [rank == lane + 128 * n for rank in ranks]
        order[n:n + 1] = sum(
            jnp.sum(jnp.where(a, slot, 0), axis=0, keepdims=True) for a, slot in zip(at, slots)
        )
        order[2 + n:3 + n] = sum(
            jnp.sum(jnp.where(a, block, 0), axis=0, keepdims=True) for a, block in zip(at, blocks)
        )
    order[4:5] = sum(
        jnp.sum((block <= lane).astype(jnp.int32), axis=0, keepdims=True) for block in blocks
    )
    order[5:8] = jnp.zeros((3, 128), jnp.int32)
    order_copy = pltpu.make_async_copy(order, order_s, local_sem.at[3])
    order_copy.start()

    phi_copy.wait()

    @pl.loop(0, NCHUNK)
    def _(j):
        cells = pl.ds(pl.multiple_of(j * CHUNK, CHUNK), CHUNK)
        for a in range(ORB_BLOCKS):
            phi_t[a * BLOCK:(a + 1) * BLOCK, cells] = phi[cells, a * BLOCK:(a + 1) * BLOCK].T

    spots = [
        (bx, by, bz)
        for bx in range(3) for by in range(3) for bz in range(3)
        if (bx, by, bz) != (1, 1, 1)
    ]
    z = w * 2 + c

    def send_density(part):
        for n, (bx, by, bz) in enumerate(spots):
            remote(
                dens.at[pl.ds(8 * part, 8)], near.at[part, n],
                near_send.at[part], near_recv.at[part],
                ((x + 5 - bx) % 4, (y + 5 - by) % 4, (z + 9 - bz) % 8),
            ).start()

    for r in range(2):
        for part in range(3):
            if r == 0:
                send, recv, span = sbufs[part], rbufs[part], pl.ds(8, NSLOT - 8)
            else:
                send, recv = s1, r1
                span = (pl.ds(4, 124), pl.ds(136, 248), pl.ds(388, 124))[part]
            remote(
                send.at[span], recv.at[span],
                out_send.at[r, part], out_recv.at[r, part], beyond(along(2, 1)),
            ).wait()

        high = GROUP * len(ROUND_TOPS[r])

        @pl.loop(0, ORB_BLOCKS)
        def _(a):
            for b in range(ORB_BLOCKS):
                p = a * ORB_BLOCKS + b
                columns = slice(b * BLOCK, (b + 1) * BLOCK)
                if r == 0:
                    for part in range(3):
                        rows = pl.ds(pl.multiple_of(a * high + part * 2 * GROUP, GROUP), 2 * GROUP)
                        lmat0[rows, columns] = rbufs[part][place_s[part, p]]
                else:
                    rank = place_s[3, p]
                    one = r1[(place_s[0, p] >> 1) + rank * (384 + (place_s[2, p] >> 1) - (place_s[0, p] >> 1))]
                    two = r1[128 + place_s[1, p]]
                    lmat1[pl.ds(pl.multiple_of(a * high, GROUP), GROUP), columns] = one
                    lmat1[pl.ds(pl.multiple_of(a * high + GROUP, GROUP), GROUP), columns] = two

        def collocate(j):
            cells = pl.ds(pl.multiple_of(j * CHUNK, CHUNK), CHUNK)
            product = jnp.dot(
                lmats[r][...], phi_t[:, cells], preferred_element_type=jnp.float32
            )
            total = jnp.zeros((GROUP, CHUNK), jnp.float32)
            for a in range(ORB_BLOCKS):
                for n, top in enumerate(ROUND_TOPS[r]):
                    into, start = a * high + n * GROUP, a * BLOCK + top
                    total = total + product[into:into + GROUP] * phi_t[
                        start:start + GROUP, cells
                    ].astype(jnp.float32)
            line = jnp.sum(total, axis=0, keepdims=True)
            if r == 0:
                dens[pl.ds(j, 1), :] = line
            else:
                dens[pl.ds(j, 1), :] += line

        if r == 0:
            pl.loop(0, NCHUNK)(collocate)
        else:
            pl.loop(0, NCHUNK // 2)(collocate)
            send_density(0)
            pl.loop(NCHUNK // 2, NCHUNK)(collocate)
            send_density(1)

    tz[0] = jnp.broadcast_to(jnp.sum(dens[...], keepdims=True), (8, 128))

    def spread(axis, held_sums):
        for offset in axes[axis]:
            place = sum(offset) if axis else offset[2] * 2 + offset[3]
            remote(
                held_sums.at[0], held_sums.at[place], tot_send.at[axis], tot_recv.at[axis],
                before(offset),
            ).start()

    def gathered(axis, held_sums):
        span = pl.ds(1, len(axes[axis]))
        remote(
            held_sums.at[span], held_sums.at[span], tot_send.at[axis], tot_recv.at[axis],
            before(axes[axis][0]),
        ).wait()
        return jnp.sum(held_sums[...], axis=0)

    spread(0, tz)
    source[1, 16:32, 256:512] = dens[...]
    for part in range(2):
        remote(
            near.at[part], near.at[part], near_send.at[part], near_recv.at[part],
            beyond((0, 0, 0, 1)),
        ).wait()
        for n, (bx, by, bz) in enumerate(spots):
            top = bx * 16 + part * 8
            source[bz, top:top + 8, by * 256:by * 256 + 256] = near[part, n]

    inner = (slice(8, 40), slice(128, 640))
    slabs = range(3)
    gain, keep = OMEGA / FINE, 1.0 - OMEGA
    wide = [source[b] for b in slabs]
    around = beside([gain * v for v in wide], 1)
    for b in slabs:
        pre[b] = (keep * gain + gain) * wide[b] + gain * around[b]
    wide = [pre[b] for b in slabs]
    around = beside(wide, 1)
    for b in slabs:
        rest = source[(b,) + inner] - FINE * wide[b][inner] + around[b][inner]
        coarse[b] = (0.5 * OMEGA / COARSE) * pair_sums(rest)
        corr[b] = coarse[b]
    ty[0] = gathered(0, tz)
    spread(1, ty)
    for _ in range(NCOARSE - 1):
        around = beside([corr[b] for b in slabs], 2)
        for b in slabs:
            corr[b] = keep * corr[b] + coarse[b] + (OMEGA / COARSE) * around[b]
    tx[0] = gathered(1, ty)
    spread(2, tx)
    for b in slabs:
        field[b] = pre[(b,) + inner] + corr[b]
    for _ in range(NPOST):
        around = beside([field[b] for b in slabs], 1)
        for b in slabs:
            field[b] = keep * field[b] + gain * (source[(b,) + inner] + around[b])
    total = gathered(2, tx)
    mean = total[0:1, 0:1] * (1.0 / TOTAL_CELLS)
    pot_ref[...] = field[1, 8:24, 128:384] - constant_response() * mean

    for q in range(4):
        send, arrived, per = sbufs[q], rbufs[q], (2, 2, 2, 4)[q]
        rows_in = [a * BLOCK + q * QUARTER for a in range(ORB_BLOCKS)]

        @pl.loop(0, NCHUNK)
        def _(j):
            cells = pl.ds(pl.multiple_of(j * CHUNK, CHUNK), CHUNK)
            line = pot_ref[pl.ds(j, 1), :]
            for a in range(ORB_BLOCKS):
                scaled[a * QUARTER:(a + 1) * QUARTER, cells] = (
                    phi_t[rows_in[a]:rows_in[a] + QUARTER, cells].astype(jnp.float32) * line
                ).astype(jnp.bfloat16)

        @pl.loop(0, ORB_BLOCKS // 2)
        def _(t):
            columns = pl.ds(pl.multiple_of(t * 2 * BLOCK, 2 * BLOCK), 2 * BLOCK)
            matrix = jnp.dot(
                scaled[...], phi[:, columns], preferred_element_type=jnp.float32
            ) * (CELLS ** -0.5)
            matrix = matrix.astype(jnp.bfloat16)
            for a in range(ORB_BLOCKS):
                for j in range(2):
                    pieces[a * ORB_BLOCKS + 2 * t + j] = matrix[
                        a * QUARTER:(a + 1) * QUARTER, j * BLOCK:(j + 1) * BLOCK
                    ]

        @pl.loop(0, NDEV)
        def _(i):
            offset = turn(i)
            k = number(offset)
            for s in range(2):
                block = pieces[own_table_s[k, s]]
                if q < 3:
                    send[2 * k + s] = block
                else:
                    send[4 * k + 2 * s] = block[:GROUP]
                    send[4 * k + 2 * s + 1] = block[GROUP:]
            span = pl.ds(per * k, per)

            @pl.when(k != 0)
            def _():
                remote(
                    send.at[span], arrived.at[span], back_send.at[q], back_recv.at[q],
                    before(offset),
                ).start()

            @pl.when(k == 0)
            def _():
                for n in range(per):
                    arrived[n] = send[n]

    order_copy.wait()
    for q in range(4):
        send, arrived, per = sbufs[q], rbufs[q], (2, 2, 2, 4)[q]
        others = pl.ds(per, per * (NDEV - 1))
        remote(
            send.at[others], arrived.at[others], back_send.at[q], back_recv.at[q],
            beyond((0, 0, 0, 1)),
        ).wait()

        def add(n, carry):
            previous, run = carry
            slot, block = order_s[n // 128, n % 128], order_s[2 + n // 128, n % 128]
            if q < 3:
                value = arrived[slot].astype(jnp.float32)
            else:
                value = jnp.concatenate(
                    [arrived[2 * slot], arrived[2 * slot + 1]], axis=0
                ).astype(jnp.float32)
            run = run * (block == previous).astype(jnp.float32) + value
            sums[n] = run
            return block, run

        lax.fori_loop(
            0, NSLOT, add, (jnp.int32(-1), jnp.zeros((QUARTER, BLOCK), jnp.float32)), unroll=4
        )

        @pl.loop(0, NNZ_DEV)
        def _(n):
            stop = order_s[4, n]
            start = jnp.where(n == 0, 0, order_s[4, jnp.maximum(n - 1, 0)])
            some = (stop > start).astype(jnp.float32)
            out_ref[n, q * QUARTER:(q + 1) * QUARTER, :] = sums[jnp.maximum(stop - 1, 0)] * some


def body(density_blocks, orbital_values, pair_index):
    phi = orbital_values.reshape(CELLS, LOCAL_ORB)
    vmem = pl.BlockSpec(memory_space=pltpu.VMEM)
    anywhere = pl.BlockSpec(memory_space=pl.ANY)
    dma = pltpu.SemaphoreType.DMA
    bf16, f32, i32 = jnp.bfloat16, jnp.float32, jnp.int32
    transit = [pltpu.VMEM((NSLOT, 2 * GROUP, BLOCK), bf16)] * 3 + [
        pltpu.VMEM((2 * NSLOT, GROUP, BLOCK), bf16)
    ]
    summed, pot = pl.pallas_call(
        main_kernel,
        out_shape=(
            jax.ShapeDtypeStruct((NNZ_DEV, BLOCK, BLOCK), f32),
            jax.ShapeDtypeStruct((16, 256), f32),
        ),
        in_specs=[vmem, vmem, anywhere],
        out_specs=(vmem, vmem),
        scratch_shapes=[
            pltpu.VMEM((CELLS, LOCAL_ORB), bf16),
            pltpu.VMEM((LOCAL_ORB, CELLS), bf16),
        ] + [
            pltpu.VMEM((3, 4 * NNZ_DEV, GROUP, BLOCK), bf16) for _ in PARTS
        ] + transit + transit + [
            pltpu.VMEM((ORB_BLOCKS * GROUP * len(tops), LOCAL_ORB), bf16) for tops in ROUND_TOPS
        ] + [
            pltpu.VMEM((ORB_BLOCKS * QUARTER, CELLS), bf16),
            pltpu.VMEM((NPAIR, QUARTER, BLOCK), bf16),
            pltpu.VMEM((NSLOT, QUARTER, BLOCK), f32),
            pltpu.VMEM((NDEV, 1, 128), i32),
            pltpu.VMEM((NDEV, 128), i32),
            pltpu.VMEM((1, 128), i32),
            pltpu.VMEM((192, 128), i32),
            pltpu.VMEM((8, 128), i32),
            pltpu.SMEM((NDEV, 128), i32),
            pltpu.SMEM((1, 128), i32),
            pltpu.SMEM((192, 128), i32),
            pltpu.SMEM((4, 128), i32),
            pltpu.SMEM((8, 128), i32),
            pltpu.VMEM((16, 256), f32),
            pltpu.VMEM((2, 26, 8, 256), f32),
            pltpu.VMEM((3, 48, 768), f32),
            pltpu.VMEM((3, 48, 768), f32),
            pltpu.VMEM((3, 32, 512), f32),
            pltpu.VMEM((3, 32, 512), f32),
            pltpu.VMEM((3, 32, 512), f32),
            pltpu.VMEM((8, 8, 128), f32),
            pltpu.VMEM((4, 8, 128), f32),
            pltpu.VMEM((4, 8, 128), f32),
            dma, dma((4,)), dma((3,)), dma((3,)), dma((3,)), dma((3,)), dma((2, 3)), dma((2, 3)),
            dma((2,)), dma((2,)), dma((3,)), dma((3,)), dma((4,)), dma((4,)),
        ],
        compiler_params=pltpu.CompilerParams(
            collective_id=0, has_side_effects=True, vmem_limit_bytes=61 * 2**20
        ),
        cost_estimate=pl.CostEstimate(
            flops=4 * CELLS * LOCAL_ORB * LOCAL_ORB, bytes_accessed=40 * 2**20, transcendentals=0
        ),
        name="collocate_solve_integrate",
    )(pair_index, density_blocks, phi)
    return summed, pot.reshape(16, 16, 16)


def solution(mesh):
    return jax.shard_map(
        body,
        mesh=mesh,
        in_specs=(
            P(("gx", "gy", "gz"), None, None),
            P("gx", "gy", "gz", None),
            P(("gx", "gy", "gz"), None),
        ),
        out_specs=(P(("gx", "gy", "gz"), None, None), P("gx", "gy", "gz")),
        check_vma=False,
    )
```

```python
import functools

import jax
import jax.numpy as jnp
from jax import lax
from jax.experimental import pallas as pl
from jax.experimental.pallas import tpu as pltpu
from jax.sharding import PartitionSpec as P

MESH = pl.DeviceIdType.MESH
ORB_BLOCKS = 10
NPAIR = 100
BLOCK = 128
NDEV = 128
NPLANE = 32
NSLOT = 256
NNZ_DEV = 32
CELLS = 4096
LOCAL_ORB = 1280
CHUNK = 256
NCHUNK = CELLS // CHUNK
TOTAL_CELLS = 524288
GROUP = 16
PIECES = ((0, 16), (16, 32), (48, 32), (80, 16), (96, 16), (112, 16))
EARLY = 26
PARTS = ((0, 16, 32), (48, 64, 80), (96, 112, 32))
ROUND_TOPS = ((0, 48, 96), (16, 64, 112), (32, 80))


OMEGA = 0.6
SCREEN = 0.05
FINE = 6.0 + SCREEN
COARSE = 6.0 + 4.0 * SCREEN
NPRE = 2
NCOARSE = 4
NPOST = 2


def constant_response():
    field = 0.0
    for _ in range(NPRE):
        field = field + OMEGA * (1.0 - (FINE - 6.0) * field) / FINE
    rest = 4.0 * (1.0 - (FINE - 6.0) * field)
    correction = 0.0
    for _ in range(NCOARSE):
        correction = correction + OMEGA * (rest - (COARSE - 6.0) * correction) / COARSE
    field = field + correction
    for _ in range(NPOST):
        field = field + OMEGA * (1.0 - (FINE - 6.0) * field) / FINE
    return field


def here():
    z = lax.axis_index("gz")
    return lax.axis_index("gx"), lax.axis_index("gy"), z // 2, z % 2


def beyond(offset):
    x, y, w, c = here()
    dx, dy, dw, dc = offset
    return (x + dx) % 4, (y + dy) % 4, ((w + dw) % 4) * 2 + (c + dc) % 2


def before(offset):
    dx, dy, dw, dc = offset
    return beyond((4 - dx, 4 - dy, 4 - dw, dc))


def offset_of(k):
    return k // 32, (k // 8) % 4, (k // 2) % 4, k % 2


def turn(i):
    a, b, e, c = i % 4, (i // 4) % 4, (i // 16) % 4, (i // 64 + i) % 2
    return a, (a + b) % 4, (a + e) % 4, c


def plane_turn(axis, i):
    a, b, c = i % 4, (i // 4) % 4, (i // 16 + i) % 2
    u, v = ((a + b) % 4, a) if axis == 1 else (a, (a + b) % 4)
    return u * 8 + v * 2 + c


def plane_offset(axis, t):
    u, v, c = t // 8, (t // 2) % 4, t % 2
    return ((0, u, v, c), (u, 0, v, c), (u, v, 0, c))[axis]


def along(axis, j):
    return tuple(j if n == axis else 0 for n in range(3)) + (0,)


def number(offset):
    dx, dy, dw, dc = offset
    return dx * 32 + dy * 8 + dw * 2 + dc


def remote(src, dst, send, recv, device):
    return pltpu.make_async_remote_copy(
        src_ref=src, dst_ref=dst, send_sem=send, recv_sem=recv,
        device_id=device, device_id_type=MESH,
    )


def beside(v, n):
    rows, lanes = v[0].shape
    zlane = lax.broadcasted_iota(jnp.int32, (rows, lanes), 1) % 16
    result = []
    for b in range(3):
        total = pltpu.roll(v[b], n, 0) + pltpu.roll(v[b], rows - n, 0)
        total = total + pltpu.roll(v[b], 16 * n, 1) + pltpu.roll(v[b], lanes - 16 * n, 1)
        up = jnp.where(
            zlane >= 16 - n,
            pltpu.roll(v[(b + 1) % 3], 16 - n, 1),
            pltpu.roll(v[b], lanes - n, 1),
        )
        down = jnp.where(
            zlane < n,
            pltpu.roll(v[(b + 2) % 3], lanes - 16 + n, 1),
            pltpu.roll(v[b], n, 1),
        )
        result.append(total + up + down)
    return result


def pair_sums(r):
    rows, lanes = r.shape
    row = lax.broadcasted_iota(jnp.int32, r.shape, 0)
    lane = lax.broadcasted_iota(jnp.int32, r.shape, 1)
    r = r + jnp.where(row % 2 == 0, pltpu.roll(r, rows - 1, 0), pltpu.roll(r, 1, 0))
    r = r + jnp.where(
        (lane // 16) % 2 == 0, pltpu.roll(r, lanes - 16, 1), pltpu.roll(r, 16, 1)
    )
    return r + jnp.where(lane % 2 == 0, pltpu.roll(r, lanes - 1, 1), pltpu.roll(r, 1, 1))


def first_last(match, value, low, high):
    first = jnp.min(jnp.where(match, value, high), axis=1, keepdims=True)
    last = jnp.max(jnp.where(match, value, low), axis=1, keepdims=True)
    return first, last


def main_kernel(
    own_ref, blocks_ref, phi_hbm,
    out_ref, pot_ref,
    phi, phi_t,
    ag_a, ag_b, ag_c,
    s0, s0c, s1, s1c, s2,
    r0, r0c, r1, r1c, r2,
    lmat0, lmat1, lmat2, scaled, pieces, sums,
    asked, own_table, own_key, send_table, order,
    own_table_s, own_key_s, send_table_s, place_s, order_s,
    dens, near, source, pre, field, coarse, corr, tz, ty, tx,
    phi_sem, local_sem, ask_send, ask_recv, ag_send, ag_recv, pass_recv, out_send, out_recv,
    near_send, near_recv, tot_send, tot_recv, back_send, back_recv,
):
    gathered_blocks = (ag_a, ag_b, ag_c)
    sbufs, rbufs = ((s0, s0c), (s1, s1c), (s2,)), ((r0, r0c), (r1, r1c), (r2,))
    lmats = (lmat0, lmat1, lmat2)
    x, y, w, c = here()
    me = x * 32 + y * 8 + w * 2 + c

    phi_copy = pltpu.make_async_copy(phi_hbm, phi, phi_sem)
    phi_copy.start()

    axes = (
        [(0, 0, k // 2, k % 2) for k in range(1, 8)],
        [(0, k, 0, 0) for k in range(1, 4)],
        [(k, 0, 0, 0) for k in range(1, 4)],
    )
    barrier = pltpu.get_barrier_semaphore()
    for offsets in axes:
        for offset in offsets:
            pl.semaphore_signal(barrier, inc=1, device_id=beyond(offset), device_id_type=MESH)

    asked[0] = jnp.zeros((1, 128), jnp.int32)
    asked[0, :, 0:NPAIR] = own_ref[...]
    pl.semaphore_wait(barrier, 13)

    def pass_on(n):
        half = NNZ_DEV // 2
        for part in range(3):
            for way, j in enumerate((1, 3)):
                held = pl.ds(j * NNZ_DEV, NNZ_DEV)
                remote(
                    gathered_blocks[part].at[n, held], gathered_blocks[part].at[n, held],
                    ag_send.at[part], ag_recv.at[n, part, way], before(along(part, 1)),
                ).wait_recv()
                remote(
                    gathered_blocks[part].at[n, pl.ds(j * NNZ_DEV + way * half, half)],
                    gathered_blocks[part].at[n, pl.ds(2 * NNZ_DEV + way * half, half)],
                    ag_send.at[part], pass_recv.at[part], before(along(part, j)),
                ).start()

    for axis, (offsets, width) in enumerate(zip(axes, (1, 8, 32))):
        for offset in offsets:
            k = number(offset)
            remote(
                asked.at[pl.ds(0, width)], asked.at[pl.ds(k, width)],
                ask_send.at[axis], ask_recv.at[axis], before(offset),
            ).start()
        if axis == 0:
            for n in range(3):
                for part, tops in enumerate(PARTS):
                    for way, j in enumerate((1, 3)):
                        remote(
                            blocks_ref.at[:, pl.ds(tops[n], GROUP), :],
                            gathered_blocks[part].at[n, pl.ds(j * NNZ_DEV, NNZ_DEV)],
                            ag_send.at[part], ag_recv.at[n, part, way], before(along(part, j)),
                        ).start()
        else:
            pass_on(axis - 1)
        if axis == 0:
            lane = lax.broadcasted_iota(jnp.int32, (NDEV, 128), 1)
            row = lax.broadcasted_iota(jnp.int32, (NDEV, 128), 0)
            own = asked[0]
            held = own >> 5
            key = (
                (((x - (held >> 5)) & 3) << 5)
                | (((y - (held >> 3)) & 3) << 3)
                | (((w - (held >> 1)) & 3) << 1)
                | ((c + held) & 1)
            )
            own_key[...] = key
            first, last = first_last((key == row) & (lane < NPAIR), lane, 0, NPAIR - 1)
            own_table[...] = jnp.where(lane == 0, first, last)
            key_copy = pltpu.make_async_copy(own_key, own_key_s, local_sem.at[0])
            key_copy.start()
            own_copy = pltpu.make_async_copy(own_table, own_table_s, local_sem.at[1])
            own_copy.start()
        elif axis == 1:
            for part, tops in enumerate(PARTS):
                for n, top in enumerate(tops):
                    gathered_blocks[part][n, 0:NNZ_DEV] = blocks_ref[:, top:top + GROUP, :]
        span = pl.ds(width, len(offsets) * width)
        remote(
            asked.at[span], asked.at[span], ask_send.at[axis], ask_recv.at[axis],
            before(offsets[0]),
        ).wait()

    pass_on(2)

    wanted = asked[:, 0, :]
    asks = (
        wanted[0:32],
        jnp.concatenate([wanted[n * 32:n * 32 + 8] for n in range(4)], axis=0),
        wanted,
    )
    for axis, base in enumerate((0, 32, 64)):
        ask = asks[axis]
        count = ask.shape[0]
        lane_n = lane[0:count]
        value = lane_n * 32 + (ask & 31)
        table = jnp.zeros((count, 128), jnp.int32)
        for j in range(4):
            holder = (
                ((x + j) % 4) * 32 + y * 8 + w * 2 + c,
                x * 32 + ((y + j) % 4) * 8 + w * 2 + c,
                x * 32 + y * 8 + ((w + j) % 4) * 2 + c,
            )[axis]
            first, last = first_last(
                ((ask >> 5) == holder) & (lane_n < NPAIR), value, 0, NNZ_DEV * 128 - 1
            )
            table = jnp.where(lane_n == 2 * j, j * NNZ_DEV + (first & 31), table)
            table = jnp.where(lane_n == 2 * j + 1, j * NNZ_DEV + (last & 31), table)
        send_table[base:base + count] = table
    table_copy = pltpu.make_async_copy(send_table, send_table_s, local_sem.at[2])
    table_copy.start()
    table_copy.wait()
    for part in range(3):
        sent = pl.ds(NNZ_DEV, 3 * NNZ_DEV)
        passed = pl.ds(2 * NNZ_DEV, NNZ_DEV)
        remote(
            gathered_blocks[part].at[:, sent], gathered_blocks[part].at[:, sent],
            ag_send.at[part], pass_recv.at[part], before(along(part, 1)),
        ).wait_send()
        remote(
            gathered_blocks[part].at[:, passed], gathered_blocks[part].at[:, passed],
            ag_send.at[part], pass_recv.at[part], before(along(part, 1)),
        ).wait_recv()

    def window(r, part, first, count):
        if r == 2:
            base, each = ((0, 4), (128, 8), (384, 4))[part]
            span = pl.ds(base + each * first, each * count)
            return s2.at[span], r2.at[span]
        span = pl.ds(8 * first, 8 * count)
        if part == 2:
            return sbufs[r][1].at[span], rbufs[r][1].at[span]
        rows = pl.ds(part * GROUP, GROUP)
        return sbufs[r][0].at[span, rows], rbufs[r][0].at[span, rows]

    def send_round(r, late, start, stop):
        @pl.loop(start, stop)
        def _(i):
            for part in range(3):
                t = plane_turn(part, i)
                line = (t, 32 + t, 64 + (t // 8) * 32 + ((t // 2) % 4) * 8 + t % 2)[part]
                send, recv = window(r, part, t, 1)
                slots = range(8)
                if r == 2:
                    slots = ((0, 2, 4, 6), range(8), (1, 3, 5, 7))[part]
                for n, slot in enumerate(slots):
                    send[n] = gathered_blocks[part][r, send_table_s[line, slot]]

                @pl.when(t != 0)
                def _():
                    remote(
                        send, recv, out_send.at[r, late, part], out_recv.at[r, part],
                        beyond(plane_offset(part, t)),
                    ).start()

                @pl.when(t == 0)
                def _():
                    for n in range(len(slots)):
                        recv[n] = send[n]

    def issue(r):
        send_round(r, 0, 0, EARLY)
        send_round(r, 1, EARLY, NPLANE)

    def wait_sent(r, late):
        for part in range(3):
            send, recv = window(r, part, *((EARLY, NPLANE - EARLY) if late else (1, EARLY - 1)))
            remote(
                send, recv, out_send.at[r, late, part], out_recv.at[r, part],
                beyond(along(2, 1)),
            ).wait_send()

    issue(0)

    key_copy.wait()
    own_copy.wait()

    @pl.loop(0, NPAIR)
    def _(p):
        k = own_key_s[0, p]
        rank = (own_table_s[k, 0] != p).astype(jnp.int32)
        dx, dy, dw = k >> 5, (k >> 3) & 3, (k >> 1) & 3
        place_s[0, p] = (k & 31) * 8 + ((4 - dx) & 3) * 2 + rank
        place_s[1, p] = (dx * 8 + (k & 7)) * 8 + ((4 - dy) & 3) * 2 + rank
        place_s[2, p] = (dx * 8 + dy * 2 + (k & 1)) * 8 + ((4 - dw) & 3) * 2 + rank
        place_s[3, p] = rank

    first, last = first_last(
        ((wanted >> 5) == me) & (lane < NPAIR), lane * 32 + (wanted & 31), -1, NNZ_DEV * 128
    )
    blocks = [
        jnp.where(last >= 0, first & 31, NNZ_DEV), jnp.where(last > first, last & 31, NNZ_DEV)
    ]
    slots = [2 * row[:, 0:1], 2 * row[:, 0:1] + 1]
    keys = [block * NSLOT + slot for block, slot in zip(blocks, slots)]
    across = [jnp.broadcast_to(key, (NDEV, 128)).T for key in keys]
    ranks = [
        sum(jnp.sum((other < key).astype(jnp.int32), axis=1, keepdims=True) for other in across)
        for key in keys
    ]
    for n in range(2):
        at = [rank == lane + 128 * n for rank in ranks]
        order[n:n + 1] = sum(
            jnp.sum(jnp.where(a, slot, 0), axis=0, keepdims=True) for a, slot in zip(at, slots)
        )
        order[2 + n:3 + n] = sum(
            jnp.sum(jnp.where(a, block, 0), axis=0, keepdims=True) for a, block in zip(at, blocks)
        )
    order[4:5] = sum(
        jnp.sum((block <= lane).astype(jnp.int32), axis=0, keepdims=True) for block in blocks
    )
    order[5:8] = jnp.zeros((3, 128), jnp.int32)
    order_copy = pltpu.make_async_copy(order, order_s, local_sem.at[3])
    order_copy.start()

    phi_copy.wait()

    @pl.loop(0, NCHUNK)
    def _(j):
        cells = pl.ds(pl.multiple_of(j * CHUNK, CHUNK), CHUNK)
        for a in range(ORB_BLOCKS):
            phi_t[a * BLOCK:(a + 1) * BLOCK, cells] = phi[cells, a * BLOCK:(a + 1) * BLOCK].T

    spots = [
        (bx, by, bz)
        for bx in range(3) for by in range(3) for bz in range(3)
        if (bx, by, bz) != (1, 1, 1)
    ]
    z = w * 2 + c

    def send_density(part):
        for n, (bx, by, bz) in enumerate(spots):
            remote(
                dens.at[pl.ds(8 * part, 8)], near.at[part, n],
                near_send.at[part], near_recv.at[part],
                ((x + 5 - bx) % 4, (y + 5 - by) % 4, (z + 9 - bz) % 8),
            ).start()

    for r in range(3):
        if r < 2:
            wait_sent(r, 0)
            issue(r + 1)
        for part in range(3):
            send, recv = window(r, part, 1, NPLANE - 1)
            remote(
                send, recv, out_send.at[r, 0, part], out_recv.at[r, part], beyond(along(2, 1))
            ).wait_recv()

        high = GROUP * len(ROUND_TOPS[r])

        @pl.loop(0, ORB_BLOCKS)
        def _(a):
            for b in range(ORB_BLOCKS):
                p = a * ORB_BLOCKS + b
                columns = slice(b * BLOCK, (b + 1) * BLOCK)
                places = [place_s[part, p] for part in range(3)]
                if r < 2:
                    both, third = rbufs[r]
                    found = (
                        both[places[0], 0:GROUP], both[places[1], GROUP:2 * GROUP],
                        third[places[2]],
                    )
                else:
                    one, two = places[0] >> 1, 384 + (places[2] >> 1)
                    found = (r2[one + place_s[3, p] * (two - one)], r2[128 + places[1]])
                for n, rows in enumerate(found):
                    top = pl.multiple_of(a * high + n * GROUP, GROUP)
                    lmats[r][pl.ds(top, GROUP), columns] = rows

        def collocate(j):
            cells = pl.ds(pl.multiple_of(j * CHUNK, CHUNK), CHUNK)
            product = jnp.dot(
                lmats[r][...], phi_t[:, cells], preferred_element_type=jnp.float32
            )
            total = jnp.zeros((GROUP, CHUNK), jnp.float32)
            for a in range(ORB_BLOCKS):
                for n, top in enumerate(ROUND_TOPS[r]):
                    into, start = a * high + n * GROUP, a * BLOCK + top
                    total = total + product[into:into + GROUP] * phi_t[
                        start:start + GROUP, cells
                    ].astype(jnp.float32)
            line = jnp.sum(total, axis=0, keepdims=True)
            if r == 0:
                dens[pl.ds(j, 1), :] = line
            else:
                dens[pl.ds(j, 1), :] += line

        def collocate_four(j):
            for n in range(4):
                collocate(4 * j + n)

        if r < 2:
            pl.loop(0, NCHUNK // 4)(collocate_four)
        else:
            pl.loop(0, NCHUNK // 8)(collocate_four)
            send_density(0)
            pl.loop(NCHUNK // 8, NCHUNK // 4)(collocate_four)
            send_density(1)

    for r in range(3):
        wait_sent(r, 1)
    wait_sent(2, 0)

    tz[0] = jnp.broadcast_to(jnp.sum(dens[...], keepdims=True), (8, 128))

    def spread(axis, held_sums):
        for offset in axes[axis]:
            place = sum(offset) if axis else offset[2] * 2 + offset[3]
            remote(
                held_sums.at[0], held_sums.at[place], tot_send.at[axis], tot_recv.at[axis],
                before(offset),
            ).start()

    def gathered(axis, held_sums):
        span = pl.ds(1, len(axes[axis]))
        remote(
            held_sums.at[span], held_sums.at[span], tot_send.at[axis], tot_recv.at[axis],
            before(axes[axis][0]),
        ).wait()
        return jnp.sum(held_sums[...], axis=0)

    spread(0, tz)
    source[1, 16:32, 256:512] = dens[...]
    for part in range(2):
        remote(
            near.at[part], near.at[part], near_send.at[part], near_recv.at[part],
            beyond((0, 0, 0, 1)),
        ).wait()
        for n, (bx, by, bz) in enumerate(spots):
            top = bx * 16 + part * 8
            source[bz, top:top + 8, by * 256:by * 256 + 256] = near[part, n]

    inner = (slice(8, 40), slice(128, 640))
    slabs = range(3)
    gain, keep = OMEGA / FINE, 1.0 - OMEGA
    wide = [source[b] for b in slabs]
    around = beside([gain * v for v in wide], 1)
    for b in slabs:
        pre[b] = (keep * gain + gain) * wide[b] + gain * around[b]
    wide = [pre[b] for b in slabs]
    around = beside(wide, 1)
    for b in slabs:
        rest = source[(b,) + inner] - FINE * wide[b][inner] + around[b][inner]
        coarse[b] = (0.5 * OMEGA / COARSE) * pair_sums(rest)
        corr[b] = coarse[b]
    ty[0] = gathered(0, tz)
    spread(1, ty)
    for _ in range(NCOARSE - 1):
        around = beside([corr[b] for b in slabs], 2)
        for b in slabs:
            corr[b] = keep * corr[b] + coarse[b] + (OMEGA / COARSE) * around[b]
    tx[0] = gathered(1, ty)
    spread(2, tx)
    for b in slabs:
        field[b] = pre[(b,) + inner] + corr[b]
    for _ in range(NPOST):
        around = beside([field[b] for b in slabs], 1)
        for b in slabs:
            field[b] = keep * field[b] + gain * (source[(b,) + inner] + around[b])
    total = gathered(2, tx)
    mean = total[0:1, 0:1] * (1.0 / TOTAL_CELLS)
    pot_ref[...] = field[1, 8:24, 128:384] - constant_response() * mean

    def transit(q):
        if q >= 4:
            return s2, r2, NSLOT * (q - 4)
        return ((s0c, r0c), (s0, r0), (s1, r1), (s1c, r1c))[q] + (0,)

    for q, (top, high) in enumerate(PIECES):
        send, arrived, base = transit(q)
        depth = ORB_BLOCKS * high

        @pl.loop(0, NCHUNK)
        def _(j):
            cells = pl.ds(pl.multiple_of(j * CHUNK, CHUNK), CHUNK)
            line = pot_ref[pl.ds(j, 1), :]
            for a in range(ORB_BLOCKS):
                rows = slice(a * BLOCK + top, a * BLOCK + top + high)
                scaled[a * high:(a + 1) * high, cells] = (
                    phi_t[rows, cells].astype(jnp.float32) * line
                ).astype(jnp.bfloat16)

        def integrate(t):
            columns = pl.ds(pl.multiple_of(t * 2 * BLOCK, 2 * BLOCK), 2 * BLOCK)
            matrix = jnp.dot(
                scaled[0:depth], phi[:, columns], preferred_element_type=jnp.float32
            ).astype(jnp.bfloat16)
            for a in range(ORB_BLOCKS):
                for j in range(2):
                    pieces[a * ORB_BLOCKS + 2 * t + j, 0:high] = matrix[
                        a * high:(a + 1) * high, j * BLOCK:(j + 1) * BLOCK
                    ]

        if q == 0:
            for t in range(ORB_BLOCKS // 2):
                integrate(t)
        else:
            pl.loop(0, ORB_BLOCKS // 2)(integrate)

        @pl.loop(0, NDEV)
        def _(i):
            offset = turn(i)
            k = number(offset)
            for s in range(2):
                send[base + 2 * k + s] = pieces[own_table_s[k, s], 0:high]
            span = pl.ds(base + 2 * k, 2)

            @pl.when(k != 0)
            def _():
                remote(
                    send.at[span], arrived.at[span], back_send.at[q], back_recv.at[q],
                    before(offset),
                ).start()

            @pl.when(k == 0)
            def _():
                for n in range(2):
                    arrived[base + n] = send[base + n]

    order_copy.wait()
    for group in ((1,), (2,), (0, 3), (4, 5)):
        for q in group:
            send, arrived, base = transit(q)
            others = pl.ds(base + 2, NSLOT - 2)
            remote(
                send.at[others], arrived.at[others], back_send.at[q], back_recv.at[q],
                beyond((0, 0, 0, 1)),
            ).wait()

        def add(n, carry):
            previous, run = carry
            slot, block = order_s[n // 128, n % 128], order_s[2 + n // 128, n % 128]
            held = []
            for q in group:
                send, arrived, base = transit(q)
                held.append(arrived[base + slot].astype(jnp.float32))
            value = held[0] if len(held) == 1 else jnp.concatenate(held, axis=0)
            run = run * (block == previous).astype(jnp.float32) + value
            sums[n] = run
            return block, run

        lax.fori_loop(
            0, NSLOT, add, (jnp.int32(-1), jnp.zeros((2 * GROUP, BLOCK), jnp.float32)), unroll=4
        )

        @pl.loop(0, NNZ_DEV)
        def _(n):
            stop = order_s[4, n]
            start = jnp.where(n == 0, 0, order_s[4, jnp.maximum(n - 1, 0)])
            some = (stop > start).astype(jnp.float32)
            total = sums[jnp.maximum(stop - 1, 0)] * some
            into = 0
            for q in group:
                top, high = PIECES[q]
                out_ref[n, top:top + high, :] = total[into:into + high]
                into += high


def body(density_blocks, orbital_values, pair_index):
    phi = orbital_values.reshape(CELLS, LOCAL_ORB)
    vmem = pl.BlockSpec(memory_space=pltpu.VMEM)
    anywhere = pl.BlockSpec(memory_space=pl.ANY)
    dma = pltpu.SemaphoreType.DMA
    bf16, f32, i32 = jnp.bfloat16, jnp.float32, jnp.int32
    transit = [
        pltpu.VMEM((NSLOT, 2 * GROUP, BLOCK), bf16), pltpu.VMEM((NSLOT, GROUP, BLOCK), bf16)
    ] * 2 + [pltpu.VMEM((2 * NSLOT, GROUP, BLOCK), bf16)]
    summed, pot = pl.pallas_call(
        main_kernel,
        out_shape=(
            jax.ShapeDtypeStruct((NNZ_DEV, BLOCK, BLOCK), f32),
            jax.ShapeDtypeStruct((16, 256), f32),
        ),
        in_specs=[vmem, vmem, anywhere],
        out_specs=(vmem, vmem),
        scratch_shapes=[
            pltpu.VMEM((CELLS, LOCAL_ORB), bf16),
            pltpu.VMEM((LOCAL_ORB, CELLS), bf16),
        ] + [
            pltpu.VMEM((3, 4 * NNZ_DEV, GROUP, BLOCK), bf16) for _ in PARTS
        ] + transit + transit + [
            pltpu.VMEM((ORB_BLOCKS * GROUP * len(tops), LOCAL_ORB), bf16) for tops in ROUND_TOPS
        ] + [
            pltpu.VMEM((2 * GROUP * ORB_BLOCKS, CELLS), bf16),
            pltpu.VMEM((NPAIR, 2 * GROUP, BLOCK), bf16),
            pltpu.VMEM((NSLOT, 2 * GROUP, BLOCK), f32),
            pltpu.VMEM((NDEV, 1, 128), i32),
            pltpu.VMEM((NDEV, 128), i32),
            pltpu.VMEM((1, 128), i32),
            pltpu.VMEM((192, 128), i32),
            pltpu.VMEM((8, 128), i32),
            pltpu.SMEM((NDEV, 128), i32),
            pltpu.SMEM((1, 128), i32),
            pltpu.SMEM((192, 128), i32),
            pltpu.SMEM((4, 128), i32),
            pltpu.SMEM((8, 128), i32),
            pltpu.VMEM((16, 256), f32),
            pltpu.VMEM((2, 26, 8, 256), f32),
            pltpu.VMEM((3, 48, 768), f32),
            pltpu.VMEM((3, 48, 768), f32),
            pltpu.VMEM((3, 32, 512), f32),
            pltpu.VMEM((3, 32, 512), f32),
            pltpu.VMEM((3, 32, 512), f32),
            pltpu.VMEM((8, 8, 128), f32),
            pltpu.VMEM((4, 8, 128), f32),
            pltpu.VMEM((4, 8, 128), f32),
            dma, dma((4,)), dma((3,)), dma((3,)), dma((3,)), dma((3, 3, 2)), dma((3,)), dma((3, 2, 3)), dma((3, 3)),
            dma((2,)), dma((2,)), dma((3,)), dma((3,)), dma((6,)), dma((6,)),
        ],
        compiler_params=pltpu.CompilerParams(
            collective_id=0, has_side_effects=True, vmem_limit_bytes=61 * 2**20
        ),
        cost_estimate=pl.CostEstimate(
            flops=4 * CELLS * LOCAL_ORB * LOCAL_ORB, bytes_accessed=40 * 2**20, transcendentals=0
        ),
        name="collocate_solve_integrate",
    )(pair_index, density_blocks, phi)
    return summed * CELLS ** -0.5, pot.reshape(16, 16, 16)


def solution(mesh):
    return jax.shard_map(
        body,
        mesh=mesh,
        in_specs=(
            P(("gx", "gy", "gz"), None, None),
            P("gx", "gy", "gz", None),
            P(("gx", "gy", "gz"), None),
        ),
        out_specs=(P(("gx", "gy", "gz"), None, None), P("gx", "gy", "gz")),
        check_vma=False,
    )
```

```python
import functools

import jax
import jax.numpy as jnp
from jax import lax
from jax.experimental import pallas as pl
from jax.experimental.pallas import tpu as pltpu
from jax.sharding import PartitionSpec as P

MESH = pl.DeviceIdType.MESH
ORB_BLOCKS = 10
NPAIR = 100
BLOCK = 128
NDEV = 128
NPLANE = 32
NSLOT = 256
NNZ_DEV = 32
CELLS = 4096
LOCAL_ORB = 1280
CHUNK = 256
NCHUNK = CELLS // CHUNK
TOTAL_CELLS = 524288
GROUP = 16
EARLY = 26
PARTS = ((0, 16, 32), (48, 64, 80), (96, 112, 32))
ROUND_TOPS = ((0, 48, 96), (16, 64, 112), (32, 80))
DIRECT = (32, 80)


OMEGA = 0.6
SCREEN = 0.05
FINE = 6.0 + SCREEN
COARSE = 6.0 + 4.0 * SCREEN
NPRE = 2
NCOARSE = 4
NPOST = 2


def constant_response():
    field = 0.0
    for _ in range(NPRE):
        field = field + OMEGA * (1.0 - (FINE - 6.0) * field) / FINE
    rest = 4.0 * (1.0 - (FINE - 6.0) * field)
    correction = 0.0
    for _ in range(NCOARSE):
        correction = correction + OMEGA * (rest - (COARSE - 6.0) * correction) / COARSE
    field = field + correction
    for _ in range(NPOST):
        field = field + OMEGA * (1.0 - (FINE - 6.0) * field) / FINE
    return field


def here():
    z = lax.axis_index("gz")
    return lax.axis_index("gx"), lax.axis_index("gy"), z // 2, z % 2


def beyond(offset):
    x, y, w, c = here()
    dx, dy, dw, dc = offset
    return (x + dx) % 4, (y + dy) % 4, ((w + dw) % 4) * 2 + (c + dc) % 2


def before(offset):
    dx, dy, dw, dc = offset
    return beyond((4 - dx, 4 - dy, 4 - dw, dc))


def offset_of(k):
    return k // 32, (k // 8) % 4, (k // 2) % 4, k % 2


def turn(i):
    a, b, e, c = i % 4, (i // 4) % 4, (i // 16) % 4, (i // 64 + i) % 2
    return a, (a + b) % 4, (a + e) % 4, c


def plane_turn(axis, i):
    a, b, c = i % 4, (i // 4) % 4, (i // 16 + i) % 2
    u, v = ((a + b) % 4, a) if axis == 1 else (a, (a + b) % 4)
    return u * 8 + v * 2 + c


def plane_offset(axis, t):
    u, v, c = t // 8, (t // 2) % 4, t % 2
    return ((0, u, v, c), (u, 0, v, c), (u, v, 0, c))[axis]


def along(axis, j):
    return tuple(j if n == axis else 0 for n in range(3)) + (0,)


def number(offset):
    dx, dy, dw, dc = offset
    return dx * 32 + dy * 8 + dw * 2 + dc


def remote(src, dst, send, recv, device):
    return pltpu.make_async_remote_copy(
        src_ref=src, dst_ref=dst, send_sem=send, recv_sem=recv,
        device_id=device, device_id_type=MESH,
    )


def beside(v, n):
    rows, lanes = v[0].shape
    zlane = lax.broadcasted_iota(jnp.int32, (rows, lanes), 1) % 16
    result = []
    for b in range(3):
        total = pltpu.roll(v[b], n, 0) + pltpu.roll(v[b], rows - n, 0)
        total = total + pltpu.roll(v[b], 16 * n, 1) + pltpu.roll(v[b], lanes - 16 * n, 1)
        up = jnp.where(
            zlane >= 16 - n,
            pltpu.roll(v[(b + 1) % 3], 16 - n, 1),
            pltpu.roll(v[b], lanes - n, 1),
        )
        down = jnp.where(
            zlane < n,
            pltpu.roll(v[(b + 2) % 3], lanes - 16 + n, 1),
            pltpu.roll(v[b], n, 1),
        )
        result.append(total + up + down)
    return result


def pair_sums(r):
    rows, lanes = r.shape
    row = lax.broadcasted_iota(jnp.int32, r.shape, 0)
    lane = lax.broadcasted_iota(jnp.int32, r.shape, 1)
    r = r + jnp.where(row % 2 == 0, pltpu.roll(r, rows - 1, 0), pltpu.roll(r, 1, 0))
    r = r + jnp.where(
        (lane // 16) % 2 == 0, pltpu.roll(r, lanes - 16, 1), pltpu.roll(r, 16, 1)
    )
    return r + jnp.where(lane % 2 == 0, pltpu.roll(r, lanes - 1, 1), pltpu.roll(r, 1, 1))


def first_last(match, value, low, high):
    first = jnp.min(jnp.where(match, value, high), axis=1, keepdims=True)
    last = jnp.max(jnp.where(match, value, low), axis=1, keepdims=True)
    return first, last


def main_kernel(
    own_ref, blocks_ref, phi_hbm,
    out_ref, pot_ref,
    phi, phi_t,
    ag_a, ag_b, ag_c,
    s0, s0c, s1, s1c, s2,
    r0, r0c, r1, r1c, r2,
    lmat0, lmat1, lmat2, scaled, pieces, sums,
    asked, asked_c, own_table, own_key, send_table, order,
    own_table_s, own_key_s, send_table_s, place_s, order_s,
    dens, near, source, pre, field, coarse, corr, tz, ty, tx,
    phi_sem, local_sem, ask_send, ask_recv, ag_send, ag_recv, pass_recv, out_send, out_recv,
    near_send, near_recv, tot_send, tot_recv, back_send, back_recv,
    relay_send, relay_recv, sum_send, sum_recv,
):
    gathered_blocks = (ag_a, ag_b, ag_c)
    sbufs, rbufs = ((s0, s0c), (s1, s1c), (s2,)), ((r0, r0c), (r1, r1c), (r2,))
    lmats = (lmat0, lmat1, lmat2)
    x, y, w, c = here()
    me = x * 32 + y * 8 + w * 2 + c

    phi_copy = pltpu.make_async_copy(phi_hbm, phi, phi_sem)
    phi_copy.start()

    axes = (
        [(0, 0, k // 2, k % 2) for k in range(1, 8)],
        [(0, k, 0, 0) for k in range(1, 4)],
        [(k, 0, 0, 0) for k in range(1, 4)],
    )
    barrier = pltpu.get_barrier_semaphore()
    for offsets in axes:
        for offset in offsets:
            pl.semaphore_signal(barrier, inc=1, device_id=beyond(offset), device_id_type=MESH)

    asked[0] = jnp.zeros((1, 128), jnp.int32)
    asked[0, :, 0:NPAIR] = own_ref[...]
    pl.semaphore_wait(barrier, 13)

    def pass_on(n):
        half = NNZ_DEV // 2
        for part in range(3):
            for way, j in enumerate((1, 3)):
                held = pl.ds(j * NNZ_DEV, NNZ_DEV)
                remote(
                    gathered_blocks[part].at[n, held], gathered_blocks[part].at[n, held],
                    ag_send.at[part], ag_recv.at[n, part, way], before(along(part, 1)),
                ).wait_recv()
                remote(
                    gathered_blocks[part].at[n, pl.ds(j * NNZ_DEV + way * half, half)],
                    gathered_blocks[part].at[n, pl.ds(2 * NNZ_DEV + way * half, half)],
                    ag_send.at[part], pass_recv.at[part], before(along(part, j)),
                ).start()

    for axis, (offsets, width) in enumerate(zip(axes, (1, 8, 32))):
        for offset in offsets:
            k = number(offset)
            remote(
                asked.at[pl.ds(0, width)], asked.at[pl.ds(k, width)],
                ask_send.at[axis], ask_recv.at[axis], before(offset),
            ).start()
        if axis == 0:
            for n in range(3):
                for part, tops in enumerate(PARTS):
                    for way, j in enumerate((1, 3)):
                        remote(
                            blocks_ref.at[:, pl.ds(tops[n], GROUP), :],
                            gathered_blocks[part].at[n, pl.ds(j * NNZ_DEV, NNZ_DEV)],
                            ag_send.at[part], ag_recv.at[n, part, way], before(along(part, j)),
                        ).start()
        else:
            pass_on(axis - 1)
        if axis == 0:
            lane = lax.broadcasted_iota(jnp.int32, (NDEV, 128), 1)
            row = lax.broadcasted_iota(jnp.int32, (NDEV, 128), 0)
            own = asked[0]
            held = own >> 5
            key = (
                (((x - (held >> 5)) & 3) << 5)
                | (((y - (held >> 3)) & 3) << 3)
                | (((w - (held >> 1)) & 3) << 1)
                | ((c + held) & 1)
            )
            own_key[...] = key
            first, last = first_last((key == row) & (lane < NPAIR), lane, 0, NPAIR - 1)
            own_table[...] = jnp.where(lane == 0, first, last)
            key_copy = pltpu.make_async_copy(own_key, own_key_s, local_sem.at[0])
            key_copy.start()
            own_copy = pltpu.make_async_copy(own_table, own_table_s, local_sem.at[1])
            own_copy.start()
        elif axis == 1:
            for part, tops in enumerate(PARTS):
                for n, top in enumerate(tops):
                    gathered_blocks[part][n, 0:NNZ_DEV] = blocks_ref[:, top:top + GROUP, :]
        span = pl.ds(width, len(offsets) * width)
        remote(
            asked.at[span], asked.at[span], ask_send.at[axis], ask_recv.at[axis],
            before(offsets[0]),
        ).wait()

    pass_on(2)

    wanted = asked[:, 0, :]
    asks = (
        wanted[0:32],
        jnp.concatenate([wanted[n * 32:n * 32 + 8] for n in range(4)], axis=0),
        wanted,
    )

    def holder_at(axis, j):
        return (
            ((x + j) % 4) * 32 + y * 8 + w * 2 + c,
            x * 32 + ((y + j) % 4) * 8 + w * 2 + c,
            x * 32 + y * 8 + ((w + j) % 4) * 2 + c,
        )[axis]

    for axis, base in enumerate((0, 32, 64)):
        ask = asks[axis]
        count = ask.shape[0]
        lane_n = lane[0:count]
        value = lane_n * 32 + (ask & 31)
        table = jnp.zeros((count, 128), jnp.int32)
        for j in range(4):
            holder = holder_at(axis, j)
            first, last = first_last(
                ((ask >> 5) == holder) & (lane_n < NPAIR), value, 0, NNZ_DEV * 128 - 1
            )
            table = jnp.where(lane_n == 2 * j, j * NNZ_DEV + (first & 31), table)
            table = jnp.where(lane_n == 2 * j + 1, j * NNZ_DEV + (last & 31), table)
        send_table[base:base + count] = table
    table_copy = pltpu.make_async_copy(send_table, send_table_s, local_sem.at[2])
    table_copy.start()
    table_copy.wait()
    for part in range(3):
        sent = pl.ds(NNZ_DEV, 3 * NNZ_DEV)
        passed = pl.ds(2 * NNZ_DEV, NNZ_DEV)
        remote(
            gathered_blocks[part].at[:, sent], gathered_blocks[part].at[:, sent],
            ag_send.at[part], pass_recv.at[part], before(along(part, 1)),
        ).wait_send()
        remote(
            gathered_blocks[part].at[:, passed], gathered_blocks[part].at[:, passed],
            ag_send.at[part], pass_recv.at[part], before(along(part, 1)),
        ).wait_recv()

    def window(r, part, first, count):
        if r == 2:
            base, each = ((0, 4), (128, 8), (384, 4))[part]
            span = pl.ds(base + each * first, each * count)
            return s2.at[span], r2.at[span]
        span = pl.ds(8 * first, 8 * count)
        if part == 2:
            return sbufs[r][1].at[span], rbufs[r][1].at[span]
        rows = pl.ds(part * GROUP, GROUP)
        return sbufs[r][0].at[span, rows], rbufs[r][0].at[span, rows]

    def send_round(r, late, start, stop):
        @pl.loop(start, stop)
        def _(i):
            for part in range(3):
                t = plane_turn(part, i)
                line = (t, 32 + t, 64 + (t // 8) * 32 + ((t // 2) % 4) * 8 + t % 2)[part]
                send, recv = window(r, part, t, 1)
                slots = range(8)
                if r == 2:
                    slots = ((0, 2, 4, 6), range(8), (1, 3, 5, 7))[part]
                for n, slot in enumerate(slots):
                    send[n] = gathered_blocks[part][r, send_table_s[line, slot]]

                @pl.when(t != 0)
                def _():
                    remote(
                        send, recv, out_send.at[r, late, part], out_recv.at[r, part],
                        beyond(plane_offset(part, t)),
                    ).start()

                @pl.when(t == 0)
                def _():
                    for n in range(len(slots)):
                        recv[n] = send[n]

    def issue(r):
        send_round(r, 0, 0, EARLY)
        send_round(r, 1, EARLY, NPLANE)

    def wait_sent(r, late):
        for part in range(3):
            send, recv = window(r, part, *((EARLY, NPLANE - EARLY) if late else (1, EARLY - 1)))
            remote(
                send, recv, out_send.at[r, late, part], out_recv.at[r, part],
                beyond(along(2, 1)),
            ).wait_send()

    issue(0)

    key_copy.wait()
    own_copy.wait()

    @pl.loop(0, NPAIR)
    def _(p):
        k = own_key_s[0, p]
        rank = (own_table_s[k, 0] != p).astype(jnp.int32)
        dx, dy, dw = k >> 5, (k >> 3) & 3, (k >> 1) & 3
        place_s[0, p] = (k & 31) * 8 + ((4 - dx) & 3) * 2 + rank
        place_s[1, p] = (dx * 8 + (k & 7)) * 8 + ((4 - dy) & 3) * 2 + rank
        place_s[2, p] = (dx * 8 + dy * 2 + (k & 1)) * 8 + ((4 - dw) & 3) * 2 + rank
        place_s[3, p] = rank

    def sort_slots(base, firsts, lasts, above, slots, none):
        blocks = [
            jnp.where(lasts >= 0, above + (firsts & 31), none),
            jnp.where(lasts > firsts, above + (lasts & 31), none),
        ]
        keys = [block * NSLOT + slot for block, slot in zip(blocks, slots)]
        across = [jnp.broadcast_to(key, (NDEV, 128)).T for key in keys]
        ranks = [
            sum(jnp.sum((other < key).astype(jnp.int32), axis=1, keepdims=True) for other in across)
            for key in keys
        ]
        for n in range(2):
            at = [rank == lane + 128 * n for rank in ranks]
            order[base + n:base + n + 1] = sum(
                jnp.sum(jnp.where(a, slot, 0), axis=0, keepdims=True) for a, slot in zip(at, slots)
            )
            order[base + 2 + n:base + 3 + n] = sum(
                jnp.sum(jnp.where(a, block, 0), axis=0, keepdims=True)
                for a, block in zip(at, blocks)
            )
        order[base + 4:base + 5] = sum(
            jnp.sum((block <= lane).astype(jnp.int32), axis=0, keepdims=True) for block in blocks
        )
        order[base + 5:base + 8] = jnp.zeros((3, 128), jnp.int32)

    count = row[:, 0:1]
    first, last = first_last(
        ((wanted >> 5) == me) & (lane < NPAIR), lane * 32 + (wanted & 31), -1, NNZ_DEV * 128
    )
    sort_slots(0, first, last, 0, (2 * count, 2 * count + 1), NNZ_DEV)
    for n in range(16):
        asked_c[2 * n:2 * n + 2] = asked[8 * n:8 * n + 2, 0, :]
    for part in range(3):
        ask = asks[part] if part < 2 else asked_c[...]
        pairs = [
            first_last(
                ((ask >> 5) == holder_at(part, j)) & (lane[0:NPLANE] < NPAIR),
                lane[0:NPLANE] * 32 + (ask & 31), -1, NNZ_DEV * 128,
            )
            for j in range(4)
        ]
        first, last = (jnp.concatenate(side, axis=0) for side in zip(*pairs))
        slot = (count & 31) * 8 + (count >> 5) * 2
        sort_slots(8 + 8 * part, first, last, count & 96, (slot, slot + 1), NDEV)
    order_copy = pltpu.make_async_copy(order, order_s, local_sem.at[3])
    order_copy.start()

    phi_copy.wait()

    @pl.loop(0, NCHUNK)
    def _(j):
        cells = pl.ds(pl.multiple_of(j * CHUNK, CHUNK), CHUNK)
        for a in range(ORB_BLOCKS):
            phi_t[a * BLOCK:(a + 1) * BLOCK, cells] = phi[cells, a * BLOCK:(a + 1) * BLOCK].T

    spots = [
        (bx, by, bz)
        for bx in range(3) for by in range(3) for bz in range(3)
        if (bx, by, bz) != (1, 1, 1)
    ]
    z = w * 2 + c

    def send_density(part):
        for n, (bx, by, bz) in enumerate(spots):
            remote(
                dens.at[pl.ds(8 * part, 8)], near.at[part, n],
                near_send.at[part], near_recv.at[part],
                ((x + 5 - bx) % 4, (y + 5 - by) % 4, (z + 9 - bz) % 8),
            ).start()

    for r in range(3):
        if r < 2:
            wait_sent(r, 0)
            issue(r + 1)
        for part in range(3):
            send, recv = window(r, part, 1, NPLANE - 1)
            remote(
                send, recv, out_send.at[r, 0, part], out_recv.at[r, part], beyond(along(2, 1))
            ).wait_recv()

        high = GROUP * len(ROUND_TOPS[r])

        @pl.loop(0, ORB_BLOCKS)
        def _(a):
            for b in range(ORB_BLOCKS):
                p = a * ORB_BLOCKS + b
                columns = slice(b * BLOCK, (b + 1) * BLOCK)
                places = [place_s[part, p] for part in range(3)]
                if r < 2:
                    both, third = rbufs[r]
                    found = (
                        both[places[0], 0:GROUP], both[places[1], GROUP:2 * GROUP],
                        third[places[2]],
                    )
                else:
                    one, two = places[0] >> 1, 384 + (places[2] >> 1)
                    found = (r2[one + place_s[3, p] * (two - one)], r2[128 + places[1]])
                for n, rows in enumerate(found):
                    top = pl.multiple_of(a * high + n * GROUP, GROUP)
                    lmats[r][pl.ds(top, GROUP), columns] = rows

        def collocate(j):
            cells = pl.ds(pl.multiple_of(j * CHUNK, CHUNK), CHUNK)
            product = jnp.dot(
                lmats[r][...], phi_t[:, cells], preferred_element_type=jnp.float32
            )
            total = jnp.zeros((GROUP, CHUNK), jnp.float32)
            for a in range(ORB_BLOCKS):
                for n, top in enumerate(ROUND_TOPS[r]):
                    into, start = a * high + n * GROUP, a * BLOCK + top
                    total = total + product[into:into + GROUP] * phi_t[
                        start:start + GROUP, cells
                    ].astype(jnp.float32)
            line = jnp.sum(total, axis=0, keepdims=True)
            if r == 0:
                dens[pl.ds(j, 1), :] = line
            else:
                dens[pl.ds(j, 1), :] += line

        def collocate_four(j):
            for n in range(4):
                collocate(4 * j + n)

        if r < 2:
            pl.loop(0, NCHUNK // 4)(collocate_four)
        else:
            pl.loop(0, NCHUNK // 8)(collocate_four)
            send_density(0)
            pl.loop(NCHUNK // 8, NCHUNK // 4)(collocate_four)
            send_density(1)

    for r in range(3):
        wait_sent(r, 1)
    wait_sent(2, 0)

    tz[0] = jnp.broadcast_to(jnp.sum(dens[...], keepdims=True), (8, 128))

    def spread(axis, held_sums):
        for offset in axes[axis]:
            place = sum(offset) if axis else offset[2] * 2 + offset[3]
            remote(
                held_sums.at[0], held_sums.at[place], tot_send.at[axis], tot_recv.at[axis],
                before(offset),
            ).start()

    def gathered(axis, held_sums):
        span = pl.ds(1, len(axes[axis]))
        remote(
            held_sums.at[span], held_sums.at[span], tot_send.at[axis], tot_recv.at[axis],
            before(axes[axis][0]),
        ).wait()
        return jnp.sum(held_sums[...], axis=0)

    spread(0, tz)
    source[1, 16:32, 256:512] = dens[...]
    for part in range(2):
        remote(
            near.at[part], near.at[part], near_send.at[part], near_recv.at[part],
            beyond((0, 0, 0, 1)),
        ).wait()
        for n, (bx, by, bz) in enumerate(spots):
            top = bx * 16 + part * 8
            source[bz, top:top + 8, by * 256:by * 256 + 256] = near[part, n]

    inner = (slice(8, 40), slice(128, 640))
    slabs = range(3)
    gain, keep = OMEGA / FINE, 1.0 - OMEGA
    wide = [source[b] for b in slabs]
    around = beside([gain * v for v in wide], 1)
    for b in slabs:
        pre[b] = (keep * gain + gain) * wide[b] + gain * around[b]
    wide = [pre[b] for b in slabs]
    around = beside(wide, 1)
    for b in slabs:
        rest = source[(b,) + inner] - FINE * wide[b][inner] + around[b][inner]
        coarse[b] = (0.5 * OMEGA / COARSE) * pair_sums(rest)
        corr[b] = coarse[b]
    ty[0] = gathered(0, tz)
    spread(1, ty)
    for _ in range(NCOARSE - 1):
        around = beside([corr[b] for b in slabs], 2)
        for b in slabs:
            corr[b] = keep * corr[b] + coarse[b] + (OMEGA / COARSE) * around[b]
    tx[0] = gathered(1, ty)
    spread(2, tx)
    for b in slabs:
        field[b] = pre[(b,) + inner] + corr[b]
    for _ in range(NPOST):
        around = beside([field[b] for b in slabs], 1)
        for b in slabs:
            field[b] = keep * field[b] + gain * (source[(b,) + inner] + around[b])
    total = gathered(2, tx)
    mean = total[0:1, 0:1] * (1.0 / TOTAL_CELLS)
    pot_ref[...] = field[1, 8:24, 128:384] - constant_response() * mean

    def integrate(tops, unroll):
        high = GROUP * len(tops)
        depth = ORB_BLOCKS * high

        @pl.loop(0, NCHUNK)
        def _(j):
            cells = pl.ds(pl.multiple_of(j * CHUNK, CHUNK), CHUNK)
            line = pot_ref[pl.ds(j, 1), :]
            for a in range(ORB_BLOCKS):
                for n, top in enumerate(tops):
                    rows = slice(a * BLOCK + top, a * BLOCK + top + GROUP)
                    scaled[a * high + n * GROUP:a * high + (n + 1) * GROUP, cells] = (
                        phi_t[rows, cells].astype(jnp.float32) * line
                    ).astype(jnp.bfloat16)

        def multiply(t):
            columns = pl.ds(pl.multiple_of(t * 2 * BLOCK, 2 * BLOCK), 2 * BLOCK)
            matrix = jnp.dot(
                scaled[0:depth], phi[:, columns], preferred_element_type=jnp.float32
            ).astype(jnp.bfloat16)
            for a in range(ORB_BLOCKS):
                for j in range(2):
                    pieces[a * ORB_BLOCKS + 2 * t + j, 0:high] = matrix[
                        a * high:(a + 1) * high, j * BLOCK:(j + 1) * BLOCK
                    ]

        if unroll:
            for t in range(ORB_BLOCKS // 2):
                multiply(t)
        else:
            pl.loop(0, ORB_BLOCKS // 2)(multiply)

    def send_direct(q):
        base = NSLOT * q

        @pl.loop(0, NDEV)
        def _(i):
            offset = turn(i)
            k = number(offset)
            for s in range(2):
                s2[base + 2 * k + s] = pieces[own_table_s[k, s], 0:GROUP]
            span = pl.ds(base + 2 * k, 2)

            @pl.when(k != 0)
            def _():
                remote(
                    s2.at[span], r2.at[span], back_send.at[q], back_recv.at[q], before(offset)
                ).start()

            @pl.when(k == 0)
            def _():
                for n in range(2):
                    r2[base + n] = s2[base + n]

    def send_relays(r):
        @pl.loop(0, NPLANE)
        def _(i):
            for part in range(3):
                t = plane_turn(part, i)
                send, recv = window(r, part, t, 1)
                for n in range(8):
                    offset = list(plane_offset(part, t))
                    offset[part] = (4 - n // 2) % 4
                    send[n] = pieces[
                        own_table_s[number(offset), n % 2], part * GROUP:(part + 1) * GROUP
                    ]

                @pl.when(t != 0)
                def _():
                    remote(
                        send, recv, relay_send.at[r, part], relay_recv.at[r, part],
                        before(plane_offset(part, t)),
                    ).start()

                @pl.when(t == 0)
                def _():
                    for n in range(8):
                        recv[n] = send[n]

    def segment_sums(takes):
        def add(n, carry):
            following = []
            for g, ((base, take), (previous, run)) in enumerate(zip(takes, carry)):
                slot = order_s[base + n // 128, n % 128]
                block = order_s[base + 2 + n // 128, n % 128]
                run = run * (block == previous).astype(jnp.float32) + take(slot).astype(jnp.float32)
                sums[n, g * GROUP:(g + 1) * GROUP] = run
                following.append((block, run))
            return tuple(following)

        empty = (jnp.int32(-1), jnp.zeros((GROUP, BLOCK), jnp.float32))
        lax.fori_loop(0, NSLOT, add, (empty,) * len(takes), unroll=4)

    def segment(base, g, n):
        stop = order_s[base + 4, n]
        start = jnp.where(n == 0, 0, order_s[base + 4, jnp.maximum(n - 1, 0)])
        some = (stop > start).astype(jnp.float32)
        return sums[jnp.maximum(stop - 1, 0), g * GROUP:(g + 1) * GROUP] * some

    def relay(r):
        for part in range(3):
            send, recv = window(r, part, 1, NPLANE - 1)
            remote(
                send, recv, relay_send.at[r, part], relay_recv.at[r, part], beyond(along(2, 1))
            ).wait_recv()
        for parts in ((0, 1), (2,)):
            takes = []
            for part in parts:
                if part < 2:
                    takes.append((8 + 8 * part, lambda slot, part=part: rbufs[r][0][
                        slot, part * GROUP:(part + 1) * GROUP]))
                else:
                    takes.append((8 + 8 * part, lambda slot: rbufs[r][1][slot]))
            segment_sums(takes)
            for g, part in enumerate(parts):
                held = gathered_blocks[part]
                if r == 1:
                    sum_copy(0, part).wait_send()

                @pl.loop(0, NNZ_DEV)
                def _(n):
                    held[r, n] = segment(8 + 8 * part, g, n).astype(jnp.bfloat16)

                @pl.loop(NNZ_DEV, 4 * NNZ_DEV)
                def _(n):
                    held[2, n] = segment(8 + 8 * part, g, n).astype(jnp.bfloat16)

                for j in (1, 3, 2):
                    span = pl.ds(j * NNZ_DEV, NNZ_DEV)
                    remote(
                        held.at[2, span], held.at[r, span],
                        sum_send.at[r, part], sum_recv.at[r, part], beyond(along(part, j)),
                    ).start()

    def sum_copy(r, part):
        span = pl.ds(NNZ_DEV, 3 * NNZ_DEV)
        return remote(
            gathered_blocks[part].at[2, span], gathered_blocks[part].at[r, span],
            sum_send.at[r, part], sum_recv.at[r, part], beyond(along(part, 1)),
        )

    def finish(r):
        for part in range(3):
            sum_copy(r, part).wait_recv()
            held, top = gathered_blocks[part], PARTS[part][r]

            @pl.loop(0, NNZ_DEV // 4)
            def _(m):
                for u in range(4):
                    n = 4 * m + u
                    out_ref[n, top:top + GROUP, :] = sum(
                        held[r, j * NNZ_DEV + n].astype(jnp.float32) for j in range(4)
                    )

    integrate(DIRECT[0:1], True)
    send_direct(0)
    for r in range(2):
        integrate(ROUND_TOPS[r], False)
        send_relays(r)
    order_copy.wait()
    relay(0)
    integrate(DIRECT[1:2], True)
    send_direct(1)
    relay(1)
    finish(0)
    for q in range(2):
        others = pl.ds(NSLOT * q + 2, NSLOT - 2)
        remote(
            s2.at[others], r2.at[others], back_send.at[q], back_recv.at[q], beyond(along(2, 1))
        ).wait()
    segment_sums([(0, lambda slot: r2[slot]), (0, lambda slot: r2[NSLOT + slot])])

    @pl.loop(0, NNZ_DEV)
    def _(n):
        for g, top in enumerate(DIRECT):
            out_ref[n, top:top + GROUP, :] = segment(0, g, n)

    finish(1)
    for part in range(3):
        sum_copy(1, part).wait_send()
        for r in range(2):
            send, recv = window(r, part, 1, NPLANE - 1)
            remote(
                send, recv, relay_send.at[r, part], relay_recv.at[r, part], beyond(along(2, 1))
            ).wait_send()


def body(density_blocks, orbital_values, pair_index):
    phi = orbital_values.reshape(CELLS, LOCAL_ORB)
    vmem = pl.BlockSpec(memory_space=pltpu.VMEM)
    anywhere = pl.BlockSpec(memory_space=pl.ANY)
    dma = pltpu.SemaphoreType.DMA
    bf16, f32, i32 = jnp.bfloat16, jnp.float32, jnp.int32
    transit = [
        pltpu.VMEM((NSLOT, 2 * GROUP, BLOCK), bf16), pltpu.VMEM((NSLOT, GROUP, BLOCK), bf16)
    ] * 2 + [pltpu.VMEM((2 * NSLOT, GROUP, BLOCK), bf16)]
    summed, pot = pl.pallas_call(
        main_kernel,
        out_shape=(
            jax.ShapeDtypeStruct((NNZ_DEV, BLOCK, BLOCK), f32),
            jax.ShapeDtypeStruct((16, 256), f32),
        ),
        in_specs=[vmem, vmem, anywhere],
        out_specs=(vmem, vmem),
        scratch_shapes=[
            pltpu.VMEM((CELLS, LOCAL_ORB), bf16),
            pltpu.VMEM((LOCAL_ORB, CELLS), bf16),
        ] + [
            pltpu.VMEM((3, 4 * NNZ_DEV, GROUP, BLOCK), bf16) for _ in PARTS
        ] + transit + transit + [
            pltpu.VMEM((ORB_BLOCKS * GROUP * len(tops), LOCAL_ORB), bf16) for tops in ROUND_TOPS
        ] + [
            pltpu.VMEM((3 * GROUP * ORB_BLOCKS, CELLS), bf16),
            pltpu.VMEM((NPAIR, 3 * GROUP, BLOCK), bf16),
            pltpu.VMEM((NSLOT, 2 * GROUP, BLOCK), f32),
            pltpu.VMEM((NDEV, 1, 128), i32),
            pltpu.VMEM((NPLANE, 128), i32),
            pltpu.VMEM((NDEV, 128), i32),
            pltpu.VMEM((1, 128), i32),
            pltpu.VMEM((192, 128), i32),
            pltpu.VMEM((32, 128), i32),
            pltpu.SMEM((NDEV, 128), i32),
            pltpu.SMEM((1, 128), i32),
            pltpu.SMEM((192, 128), i32),
            pltpu.SMEM((4, 128), i32),
            pltpu.SMEM((32, 128), i32),
            pltpu.VMEM((16, 256), f32),
            pltpu.VMEM((2, 26, 8, 256), f32),
            pltpu.VMEM((3, 48, 768), f32),
            pltpu.VMEM((3, 48, 768), f32),
            pltpu.VMEM((3, 32, 512), f32),
            pltpu.VMEM((3, 32, 512), f32),
            pltpu.VMEM((3, 32, 512), f32),
            pltpu.VMEM((8, 8, 128), f32),
            pltpu.VMEM((4, 8, 128), f32),
            pltpu.VMEM((4, 8, 128), f32),
            dma, dma((4,)), dma((3,)), dma((3,)), dma((3,)), dma((3, 3, 2)), dma((3,)), dma((3, 2, 3)), dma((3, 3)),
            dma((2,)), dma((2,)), dma((3,)), dma((3,)), dma((2,)), dma((2,)),
            dma((2, 3)), dma((2, 3)), dma((2, 3)), dma((2, 3)),
        ],
        compiler_params=pltpu.CompilerParams(
            collective_id=0, has_side_effects=True, vmem_limit_bytes=62 * 2**20
        ),
        cost_estimate=pl.CostEstimate(
            flops=4 * CELLS * LOCAL_ORB * LOCAL_ORB, bytes_accessed=40 * 2**20, transcendentals=0
        ),
        name="collocate_solve_integrate",
    )(pair_index, density_blocks, phi)
    return summed * CELLS ** -0.5, pot.reshape(16, 16, 16)


def solution(mesh):
    return jax.shard_map(
        body,
        mesh=mesh,
        in_specs=(
            P(("gx", "gy", "gz"), None, None),
            P("gx", "gy", "gz", None),
            P(("gx", "gy", "gz"), None),
        ),
        out_specs=(P(("gx", "gy", "gz"), None, None), P("gx", "gy", "gz")),
        check_vma=False,
    )
```

```python
import functools

import jax
import jax.numpy as jnp
from jax import lax
from jax.experimental import pallas as pl
from jax.experimental.pallas import tpu as pltpu
from jax.sharding import PartitionSpec as P

MESH = pl.DeviceIdType.MESH
ORB_BLOCKS = 10
NPAIR = 100
BLOCK = 128
NDEV = 128
NPLANE = 32
NSLOT = 256
NNZ_DEV = 32
CELLS = 4096
LOCAL_ORB = 1280
CHUNK = 256
NCHUNK = CELLS // CHUNK
TOTAL_CELLS = 524288
GROUP = 16
EARLY = 16
PARTS = ((0, 16, 32), (48, 64, 80), (96, 112, 32))
ROUND_TOPS = ((0, 48, 96), (16, 64, 112), (32, 80))
DIRECT = (32, 80)


OMEGA = 0.6
SCREEN = 0.05
FINE = 6.0 + SCREEN
COARSE = 6.0 + 4.0 * SCREEN
NPRE = 2
NCOARSE = 4
NPOST = 2


def constant_response():
    field = 0.0
    for _ in range(NPRE):
        field = field + OMEGA * (1.0 - (FINE - 6.0) * field) / FINE
    rest = 4.0 * (1.0 - (FINE - 6.0) * field)
    correction = 0.0
    for _ in range(NCOARSE):
        correction = correction + OMEGA * (rest - (COARSE - 6.0) * correction) / COARSE
    field = field + correction
    for _ in range(NPOST):
        field = field + OMEGA * (1.0 - (FINE - 6.0) * field) / FINE
    return field


def here():
    z = lax.axis_index("gz")
    return lax.axis_index("gx"), lax.axis_index("gy"), z // 2, z % 2


def beyond(offset):
    x, y, w, c = here()
    dx, dy, dw, dc = offset
    return (x + dx) % 4, (y + dy) % 4, ((w + dw) % 4) * 2 + (c + dc) % 2


def before(offset):
    dx, dy, dw, dc = offset
    return beyond((4 - dx, 4 - dy, 4 - dw, dc))


def offset_of(k):
    return k // 32, (k // 8) % 4, (k // 2) % 4, k % 2


def turn(i):
    a, b, e, c = i % 4, (i // 4) % 4, (i // 16) % 4, (i // 64 + i) % 2
    return a, (a + b) % 4, (a + e) % 4, c


def plane_turn(axis, i):
    a, b, c = i % 4, (i // 4) % 4, (i // 16 + i) % 2
    u, v = ((a + b) % 4, a) if axis == 1 else (a, (a + b) % 4)
    return u * 8 + v * 2 + c


def plane_offset(axis, t):
    u, v, c = t // 8, (t // 2) % 4, t % 2
    return ((0, u, v, c), (u, 0, v, c), (u, v, 0, c))[axis]


def along(axis, j):
    return tuple(j if n == axis else 0 for n in range(3)) + (0,)


def number(offset):
    dx, dy, dw, dc = offset
    return dx * 32 + dy * 8 + dw * 2 + dc


def remote(src, dst, send, recv, device):
    return pltpu.make_async_remote_copy(
        src_ref=src, dst_ref=dst, send_sem=send, recv_sem=recv,
        device_id=device, device_id_type=MESH,
    )


def beside(v, n):
    rows, lanes = v[0].shape
    zlane = lax.broadcasted_iota(jnp.int32, (rows, lanes), 1) % 16
    result = []
    for b in range(3):
        total = pltpu.roll(v[b], n, 0) + pltpu.roll(v[b], rows - n, 0)
        total = total + pltpu.roll(v[b], 16 * n, 1) + pltpu.roll(v[b], lanes - 16 * n, 1)
        up = jnp.where(
            zlane >= 16 - n,
            pltpu.roll(v[(b + 1) % 3], 16 - n, 1),
            pltpu.roll(v[b], lanes - n, 1),
        )
        down = jnp.where(
            zlane < n,
            pltpu.roll(v[(b + 2) % 3], lanes - 16 + n, 1),
            pltpu.roll(v[b], n, 1),
        )
        result.append(total + up + down)
    return result


def pair_sums(r):
    rows, lanes = r.shape
    row = lax.broadcasted_iota(jnp.int32, r.shape, 0)
    lane = lax.broadcasted_iota(jnp.int32, r.shape, 1)
    r = r + jnp.where(row % 2 == 0, pltpu.roll(r, rows - 1, 0), pltpu.roll(r, 1, 0))
    r = r + jnp.where(
        (lane // 16) % 2 == 0, pltpu.roll(r, lanes - 16, 1), pltpu.roll(r, 16, 1)
    )
    return r + jnp.where(lane % 2 == 0, pltpu.roll(r, lanes - 1, 1), pltpu.roll(r, 1, 1))


def first_last(match, value, low, high):
    first = jnp.min(jnp.where(match, value, high), axis=1, keepdims=True)
    last = jnp.max(jnp.where(match, value, low), axis=1, keepdims=True)
    return first, last


def main_kernel(
    own_ref, blocks_ref, phi_hbm,
    out_ref, pot_ref,
    phi, phi_t,
    ag_a, ag_b, ag_c,
    s0, s0c, s1, s1c, s2,
    r0, r0c, r1, r1c, r2,
    lmat0, lmat1, lmat2, scaled, pieces, sums,
    asked, asked_c, own_table, own_key, send_table, order,
    own_table_s, own_key_s, send_table_s, place_s, order_s,
    dens, near, source, pre, field, coarse, corr, tz, ty, tx,
    phi_sem, local_sem, ask_send, ask_recv, ag_send, ag_recv, pass_recv, out_send, out_recv,
    near_send, near_recv, tot_send, tot_recv, back_send, back_recv,
    relay_send, relay_recv, sum_send, sum_recv,
):
    gathered_blocks = (ag_a, ag_b, ag_c)
    sbufs, rbufs = ((s0, s0c), (s1, s1c), (s2,)), ((r0, r0c), (r1, r1c), (r2,))
    lmats = (lmat0, lmat1, lmat2)
    x, y, w, c = here()
    me = x * 32 + y * 8 + w * 2 + c

    phi_copy = pltpu.make_async_copy(phi_hbm, phi, phi_sem)
    phi_copy.start()

    axes = (
        [(0, 0, k // 2, k % 2) for k in range(1, 8)],
        [(0, k, 0, 0) for k in range(1, 4)],
        [(k, 0, 0, 0) for k in range(1, 4)],
    )
    barrier = pltpu.get_barrier_semaphore()
    for offsets in axes:
        for offset in offsets:
            pl.semaphore_signal(barrier, inc=1, device_id=beyond(offset), device_id_type=MESH)

    asked[0] = jnp.zeros((1, 128), jnp.int32)
    asked[0, :, 0:NPAIR] = own_ref[...]
    pl.semaphore_wait(barrier, 13)

    def pass_on(n):
        half = NNZ_DEV // 2
        for part in range(3):
            for way, j in enumerate((1, 3)):
                held = pl.ds(j * NNZ_DEV, NNZ_DEV)
                remote(
                    gathered_blocks[part].at[n, held], gathered_blocks[part].at[n, held],
                    ag_send.at[part], ag_recv.at[n, part, way], before(along(part, 1)),
                ).wait_recv()
                remote(
                    gathered_blocks[part].at[n, pl.ds(j * NNZ_DEV + way * half, half)],
                    gathered_blocks[part].at[n, pl.ds(2 * NNZ_DEV + way * half, half)],
                    ag_send.at[part], pass_recv.at[part], before(along(part, j)),
                ).start()

    for axis, (offsets, width) in enumerate(zip(axes, (1, 8, 32))):
        for offset in offsets:
            k = number(offset)
            remote(
                asked.at[pl.ds(0, width)], asked.at[pl.ds(k, width)],
                ask_send.at[axis], ask_recv.at[axis], before(offset),
            ).start()
        if axis == 0:
            for n in range(3):
                for part, tops in enumerate(PARTS):
                    for way, j in enumerate((1, 3)):
                        remote(
                            blocks_ref.at[:, pl.ds(tops[n], GROUP), :],
                            gathered_blocks[part].at[n, pl.ds(j * NNZ_DEV, NNZ_DEV)],
                            ag_send.at[part], ag_recv.at[n, part, way], before(along(part, j)),
                        ).start()
        else:
            pass_on(axis - 1)
        if axis == 0:
            lane = lax.broadcasted_iota(jnp.int32, (NDEV, 128), 1)
            row = lax.broadcasted_iota(jnp.int32, (NDEV, 128), 0)
            own = asked[0]
            held = own >> 5
            key = (
                (((x - (held >> 5)) & 3) << 5)
                | (((y - (held >> 3)) & 3) << 3)
                | (((w - (held >> 1)) & 3) << 1)
                | ((c + held) & 1)
            )
            own_key[...] = key
            first, last = first_last((key == row) & (lane < NPAIR), lane, 0, NPAIR - 1)
            own_table[...] = jnp.where(lane == 0, first, last)
            key_copy = pltpu.make_async_copy(own_key, own_key_s, local_sem.at[0])
            key_copy.start()
            own_copy = pltpu.make_async_copy(own_table, own_table_s, local_sem.at[1])
            own_copy.start()
        elif axis == 1:
            for part, tops in enumerate(PARTS):
                for n, top in enumerate(tops):
                    gathered_blocks[part][n, 0:NNZ_DEV] = blocks_ref[:, top:top + GROUP, :]
        span = pl.ds(width, len(offsets) * width)
        remote(
            asked.at[span], asked.at[span], ask_send.at[axis], ask_recv.at[axis],
            before(offsets[0]),
        ).wait()

    pass_on(2)

    wanted = asked[:, 0, :]
    asks = (
        wanted[0:32],
        jnp.concatenate([wanted[n * 32:n * 32 + 8] for n in range(4)], axis=0),
        wanted,
    )

    def holder_at(axis, j):
        return (
            ((x + j) % 4) * 32 + y * 8 + w * 2 + c,
            x * 32 + ((y + j) % 4) * 8 + w * 2 + c,
            x * 32 + y * 8 + ((w + j) % 4) * 2 + c,
        )[axis]

    for axis, base in enumerate((0, 32, 64)):
        ask = asks[axis]
        count = ask.shape[0]
        lane_n = lane[0:count]
        value = lane_n * 32 + (ask & 31)
        table = jnp.zeros((count, 128), jnp.int32)
        for j in range(4):
            holder = holder_at(axis, j)
            first, last = first_last(
                ((ask >> 5) == holder) & (lane_n < NPAIR), value, 0, NNZ_DEV * 128 - 1
            )
            table = jnp.where(lane_n == 2 * j, j * NNZ_DEV + (first & 31), table)
            table = jnp.where(lane_n == 2 * j + 1, j * NNZ_DEV + (last & 31), table)
        send_table[base:base + count] = table
    table_copy = pltpu.make_async_copy(send_table, send_table_s, local_sem.at[2])
    table_copy.start()
    table_copy.wait()
    for part in range(3):
        sent = pl.ds(NNZ_DEV, 3 * NNZ_DEV)
        passed = pl.ds(2 * NNZ_DEV, NNZ_DEV)
        remote(
            gathered_blocks[part].at[:, sent], gathered_blocks[part].at[:, sent],
            ag_send.at[part], pass_recv.at[part], before(along(part, 1)),
        ).wait_send()
        remote(
            gathered_blocks[part].at[:, passed], gathered_blocks[part].at[:, passed],
            ag_send.at[part], pass_recv.at[part], before(along(part, 1)),
        ).wait_recv()

    def window(r, part, first, count):
        if r == 2:
            base, each = ((0, 4), (128, 8), (384, 4))[part]
            span = pl.ds(base + each * first, each * count)
            return s2.at[span], r2.at[span]
        span = pl.ds(8 * first, 8 * count)
        if part == 2:
            return sbufs[r][1].at[span], rbufs[r][1].at[span]
        rows = pl.ds(part * GROUP, GROUP)
        return sbufs[r][0].at[span, rows], rbufs[r][0].at[span, rows]

    def send_round(r, late, start, stop):
        @pl.loop(start, stop)
        def _(i):
            for part in range(3):
                t = plane_turn(part, i)
                line = (t, 32 + t, 64 + (t // 8) * 32 + ((t // 2) % 4) * 8 + t % 2)[part]
                send, recv = window(r, part, t, 1)
                slots = range(8)
                if r == 2:
                    slots = ((0, 2, 4, 6), range(8), (1, 3, 5, 7))[part]
                for n, slot in enumerate(slots):
                    send[n] = gathered_blocks[part][r, send_table_s[line, slot]]

                @pl.when(t != 0)
                def _():
                    remote(
                        send, recv, out_send.at[r, late, part], out_recv.at[r, part],
                        beyond(plane_offset(part, t)),
                    ).start()

                @pl.when(t == 0)
                def _():
                    for n in range(len(slots)):
                        recv[n] = send[n]

    def issue(r):
        send_round(r, 0, 0, EARLY)
        send_round(r, 1, EARLY, NPLANE)

    def wait_sent(r, late):
        for part in range(3):
            send, recv = window(r, part, *((EARLY, NPLANE - EARLY) if late else (1, EARLY - 1)))
            remote(
                send, recv, out_send.at[r, late, part], out_recv.at[r, part],
                beyond(along(2, 1)),
            ).wait_send()

    issue(0)

    key_copy.wait()
    own_copy.wait()

    @pl.loop(0, NPAIR)
    def _(p):
        k = own_key_s[0, p]
        rank = (own_table_s[k, 0] != p).astype(jnp.int32)
        dx, dy, dw = k >> 5, (k >> 3) & 3, (k >> 1) & 3
        place_s[0, p] = (k & 31) * 8 + ((4 - dx) & 3) * 2 + rank
        place_s[1, p] = (dx * 8 + (k & 7)) * 8 + ((4 - dy) & 3) * 2 + rank
        place_s[2, p] = (dx * 8 + dy * 2 + (k & 1)) * 8 + ((4 - dw) & 3) * 2 + rank
        place_s[3, p] = rank

    def sort_slots(base, firsts, lasts, above, slots, none):
        blocks = [
            jnp.where(lasts >= 0, above + (firsts & 31), none),
            jnp.where(lasts > firsts, above + (lasts & 31), none),
        ]
        keys = [block * NSLOT + slot for block, slot in zip(blocks, slots)]
        across = [jnp.broadcast_to(key, (NDEV, 128)).T for key in keys]
        ranks = [
            sum(jnp.sum((other < key).astype(jnp.int32), axis=1, keepdims=True) for other in across)
            for key in keys
        ]
        for n in range(2):
            at = [rank == lane + 128 * n for rank in ranks]
            order[base + n:base + n + 1] = sum(
                jnp.sum(jnp.where(a, slot, 0), axis=0, keepdims=True) for a, slot in zip(at, slots)
            )
            order[base + 2 + n:base + 3 + n] = sum(
                jnp.sum(jnp.where(a, block, 0), axis=0, keepdims=True)
                for a, block in zip(at, blocks)
            )
        order[base + 4:base + 5] = sum(
            jnp.sum((block <= lane).astype(jnp.int32), axis=0, keepdims=True) for block in blocks
        )
        order[base + 5:base + 8] = jnp.zeros((3, 128), jnp.int32)

    count = row[:, 0:1]
    first, last = first_last(
        ((wanted >> 5) == me) & (lane < NPAIR), lane * 32 + (wanted & 31), -1, NNZ_DEV * 128
    )
    sort_slots(0, first, last, 0, (2 * count, 2 * count + 1), NNZ_DEV)
    for n in range(16):
        asked_c[2 * n:2 * n + 2] = asked[8 * n:8 * n + 2, 0, :]
    for part in range(3):
        ask = asks[part] if part < 2 else asked_c[...]
        pairs = [
            first_last(
                ((ask >> 5) == holder_at(part, j)) & (lane[0:NPLANE] < NPAIR),
                lane[0:NPLANE] * 32 + (ask & 31), -1, NNZ_DEV * 128,
            )
            for j in range(4)
        ]
        first, last = (jnp.concatenate(side, axis=0) for side in zip(*pairs))
        slot = (count & 31) * 8 + (count >> 5) * 2
        sort_slots(8 + 8 * part, first, last, count & 96, (slot, slot + 1), NDEV)
    order_copy = pltpu.make_async_copy(order, order_s, local_sem.at[3])
    order_copy.start()

    phi_copy.wait()

    @pl.loop(0, NCHUNK)
    def _(j):
        cells = pl.ds(pl.multiple_of(j * CHUNK, CHUNK), CHUNK)
        for a in range(ORB_BLOCKS):
            phi_t[a * BLOCK:(a + 1) * BLOCK, cells] = phi[cells, a * BLOCK:(a + 1) * BLOCK].T

    spots = [
        (bx, by, bz)
        for bx in range(3) for by in range(3) for bz in range(3)
        if (bx, by, bz) != (1, 1, 1)
    ]
    z = w * 2 + c

    def send_density(part):
        for n, (bx, by, bz) in enumerate(spots):
            remote(
                dens.at[pl.ds(8 * part, 8)], near.at[part, n],
                near_send.at[part], near_recv.at[part],
                ((x + 5 - bx) % 4, (y + 5 - by) % 4, (z + 9 - bz) % 8),
            ).start()

    for r in range(3):
        if r < 2:
            wait_sent(r, 0)
            issue(r + 1)
        for part in range(3):
            send, recv = window(r, part, 1, NPLANE - 1)
            remote(
                send, recv, out_send.at[r, 0, part], out_recv.at[r, part], beyond(along(2, 1))
            ).wait_recv()

        high = GROUP * len(ROUND_TOPS[r])

        @pl.loop(0, ORB_BLOCKS)
        def _(a):
            for b in range(ORB_BLOCKS):
                p = a * ORB_BLOCKS + b
                columns = slice(b * BLOCK, (b + 1) * BLOCK)
                places = [place_s[part, p] for part in range(3)]
                if r < 2:
                    both, third = rbufs[r]
                    found = (
                        both[places[0], 0:GROUP], both[places[1], GROUP:2 * GROUP],
                        third[places[2]],
                    )
                else:
                    one, two = places[0] >> 1, 384 + (places[2] >> 1)
                    found = (r2[one + place_s[3, p] * (two - one)], r2[128 + places[1]])
                for n, rows in enumerate(found):
                    top = pl.multiple_of(a * high + n * GROUP, GROUP)
                    lmats[r][pl.ds(top, GROUP), columns] = rows

        def collocate(j):
            cells = pl.ds(pl.multiple_of(j * CHUNK, CHUNK), CHUNK)
            product = jnp.dot(
                lmats[r][...], phi_t[:, cells], preferred_element_type=jnp.float32
            )
            total = jnp.zeros((GROUP, CHUNK), jnp.float32)
            for a in range(ORB_BLOCKS):
                for n, top in enumerate(ROUND_TOPS[r]):
                    into, start = a * high + n * GROUP, a * BLOCK + top
                    total = total + product[into:into + GROUP] * phi_t[
                        start:start + GROUP, cells
                    ].astype(jnp.float32)
            line = jnp.sum(total, axis=0, keepdims=True)
            if r == 0:
                dens[pl.ds(j, 1), :] = line
            else:
                dens[pl.ds(j, 1), :] += line

        def collocate_four(j):
            for n in range(4):
                collocate(4 * j + n)

        if r < 2:
            pl.loop(0, NCHUNK // 4)(collocate_four)
        else:
            pl.loop(0, NCHUNK // 8)(collocate_four)
            send_density(0)
            pl.loop(NCHUNK // 8, NCHUNK // 4)(collocate_four)
            send_density(1)

    for r in range(3):
        wait_sent(r, 1)
    wait_sent(2, 0)

    tz[0] = jnp.broadcast_to(jnp.sum(dens[...], keepdims=True), (8, 128))

    def spread(axis, held_sums):
        for offset in axes[axis]:
            place = sum(offset) if axis else offset[2] * 2 + offset[3]
            remote(
                held_sums.at[0], held_sums.at[place], tot_send.at[axis], tot_recv.at[axis],
                before(offset),
            ).start()

    def gathered(axis, held_sums):
        span = pl.ds(1, len(axes[axis]))
        remote(
            held_sums.at[span], held_sums.at[span], tot_send.at[axis], tot_recv.at[axis],
            before(axes[axis][0]),
        ).wait()
        return jnp.sum(held_sums[...], axis=0)

    spread(0, tz)
    source[1, 16:32, 256:512] = dens[...]
    for part in range(2):
        remote(
            near.at[part], near.at[part], near_send.at[part], near_recv.at[part],
            beyond((0, 0, 0, 1)),
        ).wait()
        for n, (bx, by, bz) in enumerate(spots):
            top = bx * 16 + part * 8
            source[bz, top:top + 8, by * 256:by * 256 + 256] = near[part, n]

    inner = (slice(8, 40), slice(128, 640))
    slabs = range(3)
    gain, keep = OMEGA / FINE, 1.0 - OMEGA
    wide = [source[b] for b in slabs]
    around = beside([gain * v for v in wide], 1)
    for b in slabs:
        pre[b] = (keep * gain + gain) * wide[b] + gain * around[b]
    wide = [pre[b] for b in slabs]
    around = beside(wide, 1)
    for b in slabs:
        rest = source[(b,) + inner] - FINE * wide[b][inner] + around[b][inner]
        coarse[b] = (0.5 * OMEGA / COARSE) * pair_sums(rest)
        corr[b] = coarse[b]
    ty[0] = gathered(0, tz)
    spread(1, ty)
    for _ in range(NCOARSE - 1):
        around = beside([corr[b] for b in slabs], 2)
        for b in slabs:
            corr[b] = keep * corr[b] + coarse[b] + (OMEGA / COARSE) * around[b]
    tx[0] = gathered(1, ty)
    spread(2, tx)
    for b in slabs:
        field[b] = pre[(b,) + inner] + corr[b]
    for _ in range(NPOST):
        around = beside([field[b] for b in slabs], 1)
        for b in slabs:
            field[b] = keep * field[b] + gain * (source[(b,) + inner] + around[b])
    total = gathered(2, tx)
    mean = total[0:1, 0:1] * (1.0 / TOTAL_CELLS)
    pot_ref[...] = field[1, 8:24, 128:384] - constant_response() * mean

    def integrate(tops, unroll):
        high = GROUP * len(tops)
        depth = ORB_BLOCKS * high

        @pl.loop(0, NCHUNK)
        def _(j):
            cells = pl.ds(pl.multiple_of(j * CHUNK, CHUNK), CHUNK)
            line = pot_ref[pl.ds(j, 1), :]
            for a in range(ORB_BLOCKS):
                for n, top in enumerate(tops):
                    rows = slice(a * BLOCK + top, a * BLOCK + top + GROUP)
                    scaled[a * high + n * GROUP:a * high + (n + 1) * GROUP, cells] = (
                        phi_t[rows, cells].astype(jnp.float32) * line
                    ).astype(jnp.bfloat16)

        def multiply(t):
            columns = pl.ds(pl.multiple_of(t * 2 * BLOCK, 2 * BLOCK), 2 * BLOCK)
            matrix = jnp.dot(
                scaled[0:depth], phi[:, columns], preferred_element_type=jnp.float32
            ).astype(jnp.bfloat16)
            for a in range(ORB_BLOCKS):
                for j in range(2):
                    pieces[a * ORB_BLOCKS + 2 * t + j, 0:high] = matrix[
                        a * high:(a + 1) * high, j * BLOCK:(j + 1) * BLOCK
                    ]

        if unroll:
            for t in range(ORB_BLOCKS // 2):
                multiply(t)
        else:
            pl.loop(0, ORB_BLOCKS // 2)(multiply)

    def send_direct(q):
        base = NSLOT * q

        @pl.loop(0, NDEV)
        def _(i):
            offset = turn(i)
            k = number(offset)
            for s in range(2):
                s2[base + 2 * k + s] = pieces[own_table_s[k, s], 0:GROUP]
            span = pl.ds(base + 2 * k, 2)

            @pl.when(k != 0)
            def _():
                remote(
                    s2.at[span], r2.at[span], back_send.at[q], back_recv.at[q], before(offset)
                ).start()

            @pl.when(k == 0)
            def _():
                for n in range(2):
                    r2[base + n] = s2[base + n]

    def send_relays(r):
        @pl.loop(0, NPLANE)
        def _(i):
            for part in range(3):
                t = plane_turn(part, i)
                send, recv = window(r, part, t, 1)
                for n in range(8):
                    offset = list(plane_offset(part, t))
                    offset[part] = (4 - n // 2) % 4
                    send[n] = pieces[
                        own_table_s[number(offset), n % 2], part * GROUP:(part + 1) * GROUP
                    ]

                @pl.when(t != 0)
                def _():
                    remote(
                        send, recv, relay_send.at[r, part], relay_recv.at[r, part],
                        before(plane_offset(part, t)),
                    ).start()

                @pl.when(t == 0)
                def _():
                    for n in range(8):
                        recv[n] = send[n]

    def segment_sums(takes):
        def add(n, carry):
            following = []
            for g, ((base, take), (previous, run)) in enumerate(zip(takes, carry)):
                slot = order_s[base + n // 128, n % 128]
                block = order_s[base + 2 + n // 128, n % 128]
                run = run * (block == previous).astype(jnp.float32) + take(slot).astype(jnp.float32)
                sums[n, g * GROUP:(g + 1) * GROUP] = run
                following.append((block, run))
            return tuple(following)

        empty = (jnp.int32(-1), jnp.zeros((GROUP, BLOCK), jnp.float32))
        lax.fori_loop(0, NSLOT, add, (empty,) * len(takes), unroll=4)

    def segment(base, g, n):
        stop = order_s[base + 4, n]
        start = jnp.where(n == 0, 0, order_s[base + 4, jnp.maximum(n - 1, 0)])
        some = (stop > start).astype(jnp.float32)
        return sums[jnp.maximum(stop - 1, 0), g * GROUP:(g + 1) * GROUP] * some

    def relay(r):
        for part in range(3):
            send, recv = window(r, part, 1, NPLANE - 1)
            remote(
                send, recv, relay_send.at[r, part], relay_recv.at[r, part], beyond(along(2, 1))
            ).wait_recv()
        for parts in ((0, 1), (2,)):
            takes = []
            for part in parts:
                if part < 2:
                    takes.append((8 + 8 * part, lambda slot, part=part: rbufs[r][0][
                        slot, part * GROUP:(part + 1) * GROUP]))
                else:
                    takes.append((8 + 8 * part, lambda slot: rbufs[r][1][slot]))
            segment_sums(takes)
            for g, part in enumerate(parts):
                held = gathered_blocks[part]
                if r == 1:
                    sum_copy(0, part).wait_send()

                @pl.loop(0, NNZ_DEV)
                def _(n):
                    held[r, n] = segment(8 + 8 * part, g, n).astype(jnp.bfloat16)

                @pl.loop(NNZ_DEV, 4 * NNZ_DEV)
                def _(n):
                    held[2, n] = segment(8 + 8 * part, g, n).astype(jnp.bfloat16)

                for j in (1, 3, 2):
                    span = pl.ds(j * NNZ_DEV, NNZ_DEV)
                    remote(
                        held.at[2, span], held.at[r, span],
                        sum_send.at[r, part], sum_recv.at[r, part], beyond(along(part, j)),
                    ).start()

    def sum_copy(r, part):
        span = pl.ds(NNZ_DEV, 3 * NNZ_DEV)
        return remote(
            gathered_blocks[part].at[2, span], gathered_blocks[part].at[r, span],
            sum_send.at[r, part], sum_recv.at[r, part], beyond(along(part, 1)),
        )

    def finish(r):
        for part in range(3):
            sum_copy(r, part).wait_recv()
            held, top = gathered_blocks[part], PARTS[part][r]

            @pl.loop(0, NNZ_DEV // 4)
            def _(m):
                for u in range(4):
                    n = 4 * m + u
                    out_ref[n, top:top + GROUP, :] = sum(
                        held[r, j * NNZ_DEV + n].astype(jnp.float32) for j in range(4)
                    )

    integrate(DIRECT[0:1], True)
    send_direct(0)
    for r in range(2):
        integrate(ROUND_TOPS[r], False)
        send_relays(r)
    order_copy.wait()
    integrate(DIRECT[1:2], True)
    relay(0)
    send_direct(1)
    relay(1)
    finish(0)
    for q in range(2):
        others = pl.ds(NSLOT * q + 2, NSLOT - 2)
        remote(
            s2.at[others], r2.at[others], back_send.at[q], back_recv.at[q], beyond(along(2, 1))
        ).wait()
    segment_sums([(0, lambda slot: r2[slot]), (0, lambda slot: r2[NSLOT + slot])])

    @pl.loop(0, NNZ_DEV)
    def _(n):
        for g, top in enumerate(DIRECT):
            out_ref[n, top:top + GROUP, :] = segment(0, g, n)

    finish(1)
    for part in range(3):
        sum_copy(1, part).wait_send()
        for r in range(2):
            send, recv = window(r, part, 1, NPLANE - 1)
            remote(
                send, recv, relay_send.at[r, part], relay_recv.at[r, part], beyond(along(2, 1))
            ).wait_send()


def body(density_blocks, orbital_values, pair_index):
    phi = orbital_values.reshape(CELLS, LOCAL_ORB)
    vmem = pl.BlockSpec(memory_space=pltpu.VMEM)
    anywhere = pl.BlockSpec(memory_space=pl.ANY)
    dma = pltpu.SemaphoreType.DMA
    bf16, f32, i32 = jnp.bfloat16, jnp.float32, jnp.int32
    transit = [
        pltpu.VMEM((NSLOT, 2 * GROUP, BLOCK), bf16), pltpu.VMEM((NSLOT, GROUP, BLOCK), bf16)
    ] * 2 + [pltpu.VMEM((2 * NSLOT, GROUP, BLOCK), bf16)]
    summed, pot = pl.pallas_call(
        main_kernel,
        out_shape=(
            jax.ShapeDtypeStruct((NNZ_DEV, BLOCK, BLOCK), f32),
            jax.ShapeDtypeStruct((16, 256), f32),
        ),
        in_specs=[vmem, vmem, anywhere],
        out_specs=(vmem, vmem),
        scratch_shapes=[
            pltpu.VMEM((CELLS, LOCAL_ORB), bf16),
            pltpu.VMEM((LOCAL_ORB, CELLS), bf16),
        ] + [
            pltpu.VMEM((3, 4 * NNZ_DEV, GROUP, BLOCK), bf16) for _ in PARTS
        ] + transit + transit + [
            pltpu.VMEM((ORB_BLOCKS * GROUP * len(tops), LOCAL_ORB), bf16) for tops in ROUND_TOPS
        ] + [
            pltpu.VMEM((3 * GROUP * ORB_BLOCKS, CELLS), bf16),
            pltpu.VMEM((NPAIR, 3 * GROUP, BLOCK), bf16),
            pltpu.VMEM((NSLOT, 2 * GROUP, BLOCK), f32),
            pltpu.VMEM((NDEV, 1, 128), i32),
            pltpu.VMEM((NPLANE, 128), i32),
            pltpu.VMEM((NDEV, 128), i32),
            pltpu.VMEM((1, 128), i32),
            pltpu.VMEM((192, 128), i32),
            pltpu.VMEM((32, 128), i32),
            pltpu.SMEM((NDEV, 128), i32),
            pltpu.SMEM((1, 128), i32),
            pltpu.SMEM((192, 128), i32),
            pltpu.SMEM((4, 128), i32),
            pltpu.SMEM((32, 128), i32),
            pltpu.VMEM((16, 256), f32),
            pltpu.VMEM((2, 26, 8, 256), f32),
            pltpu.VMEM((3, 48, 768), f32),
            pltpu.VMEM((3, 48, 768), f32),
            pltpu.VMEM((3, 32, 512), f32),
            pltpu.VMEM((3, 32, 512), f32),
            pltpu.VMEM((3, 32, 512), f32),
            pltpu.VMEM((8, 8, 128), f32),
            pltpu.VMEM((4, 8, 128), f32),
            pltpu.VMEM((4, 8, 128), f32),
            dma, dma((4,)), dma((3,)), dma((3,)), dma((3,)), dma((3, 3, 2)), dma((3,)), dma((3, 2, 3)), dma((3, 3)),
            dma((2,)), dma((2,)), dma((3,)), dma((3,)), dma((2,)), dma((2,)),
            dma((2, 3)), dma((2, 3)), dma((2, 3)), dma((2, 3)),
        ],
        compiler_params=pltpu.CompilerParams(
            collective_id=0, has_side_effects=True, vmem_limit_bytes=62 * 2**20
        ),
        cost_estimate=pl.CostEstimate(
            flops=4 * CELLS * LOCAL_ORB * LOCAL_ORB, bytes_accessed=40 * 2**20, transcendentals=0
        ),
        name="collocate_solve_integrate",
    )(pair_index, density_blocks, phi)
    return summed * CELLS ** -0.5, pot.reshape(16, 16, 16)


def solution(mesh):
    return jax.shard_map(
        body,
        mesh=mesh,
        in_specs=(
            P(("gx", "gy", "gz"), None, None),
            P("gx", "gy", "gz", None),
            P(("gx", "gy", "gz"), None),
        ),
        out_specs=(P(("gx", "gy", "gz"), None, None), P("gx", "gy", "gz")),
        check_vma=False,
    )
```
